32 devices in a mesh: tx: 8 (over y, x, core), ty: 4 (over z).
Axes of the slice: x: 2, y: 2, z: 4, core: 2. Of those that a mesh axis runs over, the one named last changes fastest.
Arguments:
- pressure: float32 [128, 64, 1], P('tx', 'ty'), may hold values from -6 to 6
- mobility: float32 [11, 128, 64, 1], P(None, 'tx', 'ty'), may hold values from 0.05 to 1
- mob_deriv: float32 [121, 128, 64, 1], P(None, 'tx', 'ty'), may hold values from -6 to 6
- accum: float32 [121, 128, 64, 1], P(None, 'tx', 'ty'), may hold values from -6 to 6
- trans: float32 [3, 128, 64, 1], P(None, 'tx', 'ty'), may hold values from 0.1 to 2
- upwind: int32 [3, 128, 64, 1], P(None, 'tx', 'ty'), may hold values 0 or 1
- fault_send: int32 [32, 32, 2], P(('tx', 'ty')), may hold values from 0 to 255
- fault_cell: int32 [32, 64], P(('tx', 'ty')), may hold values from 0 to 255, as said below
- fault_slot: int32 [32, 64], P(('tx', 'ty')), may hold values from 0 to 63, each once within a row
- fault_trans: float32 [32, 64], P(('tx', 'ty')), may hold values from 0.1 to 2
- fault_up: int32 [32, 64], P(('tx', 'ty')), may hold values 0 or 1
- cell_owner: int32 [8192, 1], P(('tx', 'ty')), may hold values from 0 to 31; in each aligned block of 256 rows (0 to 255, 256 to 511, ...) at most 16 rows name the same one
Outputs:
- relaid: bfloat16 [16384, 8, 256], P(('tx', 'ty'))
The draws below stay inside these ranges and needn't reach their ends.
Inputs may be any that keep to these rules, and one draw needn't show every extreme that they name: `fault_cell`: each tile's 64 entries are distinct local cells. `fault_slot`: each tile's row is a permutation of the received slots. `fault_send`: local cell indices of the sending tile. `cell_owner`: among the cells of one tile (aligned blocks of 256 in global cell order) at most 16 have the same owner.
All inputs are finite; a program needn't handle non-finite values. No bound on the sum of `upwind` or of `fault_up` on one device may be relied on, other than what follows from the above.
Results may differ from the reference program's by a relative error of at most 0.0045.
Values may be sent and summed in bfloat16 or wider, within the bound.
A program may use at most 64 MiB of HBM per device.

```python
import math
import jax
import jax.numpy as jnp
import numpy as np

NEQ = 11
PAD = 16
GX = 16
GY = 16
NZ = 1
FCAP = 2
NDEV = 32
CELLS_DEV = 256
NFAULT = 64
CAPR = 16
NX = 128
NY = 64
CELLS = 8192
N_TX = 8
N_TY = 4


def draw_fault_cell(key, part):
    keys = jax.random.split(key, NDEV)
    picks = jax.vmap(lambda single: jax.random.permutation(single, CELLS_DEV)[:NFAULT])(keys)
    return picks.astype(jnp.int32)


def set_ends(entries, key, low, top_value):
    longest = entries.shape.index(max(entries.shape))
    spots = []
    for shift in (0, 1):
        where = [jax.random.randint(jax.random.fold_in(key, axis), (), 0, length) for axis, length in enumerate(entries.shape)]
        where[longest] = (where[longest] + shift) % entries.shape[longest]
        spots.append(tuple(where))
    return entries.at[spots[0]].set(low).at[spots[1]].set(top_value)


def level_of(own_key, shape, shards, smallest, high):
    loudness = 1.0
    for position, blocks in shards:
        steps = jax.random.uniform(jax.random.fold_in(jax.random.fold_in(own_key, 6), position), (blocks,), jnp.float32, smallest / len(shards), high / len(shards))
        loudness = loudness * jnp.repeat(jnp.exp(steps), shape[position] // blocks).reshape((-1,) + (1,) * (len(shape) - 1 - position))
    return loudness


def shared_out(stream_key, own, number, rows, amount, top, limit, skew):
    order = jax.random.permutation(stream_key, amount)
    heavy_load, usual = shares(amount, rows * top, limit, skew, True), shares(amount, rows * top, limit, skew, False)
    places = jnp.arange(amount)

    def named(tallies, turn):
        used = int((tallies > 0).sum())
        fixed = max(1, used // 4)
        shifted = fixed + (places - fixed + turn * (used - fixed)) % max(1, amount - fixed)
        return jnp.zeros((amount,), jnp.int32).at[order[jnp.where(places < fixed, places, shifted)]].set(jnp.asarray(tallies, jnp.int32))

    tallies = jnp.where(number % 4 == 0, named(heavy_load, number // 4), named(usual, number - number // 4 - 1))
    mixed = jax.random.permutation(jax.random.fold_in(own, 3), amount)
    giver, sink = mixed[0:amount // 2 * 2:2], mixed[1:amount // 2 * 2:2]
    margin = jnp.minimum(tallies[giver] - 1, limit - tallies[sink]) // 2
    margin = jnp.where((giver == order[0]) | (sink == order[0]) | (tallies[sink] == 0), 0, jnp.maximum(margin, 0))
    shifted = jax.random.randint(jax.random.fold_in(own, 4), (amount // 2,), 0, 1 << 20) % (margin + 1)
    tallies = tallies.at[giver].add(-shifted).at[sink].add(shifted)
    items = jnp.searchsorted(jnp.cumsum(tallies), jnp.arange(rows * top), side="right").astype(jnp.int32)
    table = items.reshape(top, rows).T
    table = table[jax.random.permutation(jax.random.fold_in(own, 1), rows)]
    turn = jax.random.randint(jax.random.fold_in(own, 2), (rows, 1), 0, top)
    return jnp.take_along_axis(table, (jnp.arange(top)[None, :] + turn) % top, axis=1)


def shares(count, total, limit, lean, full):
    weights = [(1 << 20) // math.isqrt(rank ** lean) + 1 for rank in range(1, count + 1)]
    largest = limit if full else min(limit, max(-(-total // count), total * weights[0] // sum(weights)))
    least = 1 if total - largest >= count - 1 else 0
    given, spare = [largest] + [least] * (count - 1), total - largest - least * (count - 1)
    while spare > 0:
        candidates = [i for i in range(1, count) if given[i] < largest] or [i for i in range(1, count) if given[i] < limit]
        whole, remaining = sum([weights[i] for i in candidates]), spare
        for i in candidates:
            extra = min(limit - given[i], max(1, remaining * weights[i] // whole), spare)
            given[i] = given[i] + extra
            spare = spare - extra
    return np.array(given)


def noise(own_key, extent, deviation, most, cuts=(), kind=jnp.bfloat16):
    values = deviation * jax.random.normal(own_key, extent, jnp.float32)
    if cuts:
        values = values * level_of(own_key, extent, cuts, -0.22, 0.18)
    return jnp.clip(values, -most, most).astype(kind)


def setup_inputs(seed: int = 0) -> dict:
    key_list = jax.random.split(jax.random.key(seed), 13)
    pressure = noise(key_list[0], (NX, NY, NZ), 1.0, 6.0, ((0, 8), (1, 4)), jnp.float32)
    mobility = jnp.clip(jnp.exp(math.log(1.0) - 2.9957323 * jax.random.uniform(key_list[1], (NEQ, NX, NY, NZ), jnp.float32) ** level_of(key_list[1], (NEQ, NX, NY, NZ), ((1, 8), (2, 4)), -0.2, 0.2)), 0.05, 1.0)
    mob_deriv = noise(key_list[2], (NEQ * NEQ, NX, NY, NZ), 1.0, 6.0, ((1, 8), (2, 4)), jnp.float32)
    accum = noise(key_list[3], (NEQ * NEQ, NX, NY, NZ), 1.0, 6.0, ((1, 8), (2, 4)), jnp.float32)
    trans = jnp.clip(jnp.exp(math.log(2.0) - 2.9957323 * jax.random.uniform(key_list[4], (3, NX, NY, NZ), jnp.float32) ** level_of(key_list[4], (3, NX, NY, NZ), ((1, 8), (2, 4)), -0.2, 0.2)), 0.1, 2.0)
    upwind = set_ends((jax.random.randint(key_list[5], (3, NX, NY, NZ), 0, 2) < 1).astype(jnp.int32), jax.random.fold_in(key_list[5], 1), 0, 1)
    fault_send = set_ends(jax.random.randint(key_list[6], (NDEV, NDEV, FCAP), 0, CELLS_DEV), jax.random.fold_in(key_list[6], 1), 0, CELLS_DEV - 1).astype(jnp.int32)
    fault_cell = draw_fault_cell(jax.random.fold_in(key_list[12], 71), 0)
    fault_slot = jax.vmap(lambda own: jax.random.permutation(own, NFAULT))(jax.random.split(key_list[8], NDEV)).reshape((NDEV, NFAULT)).astype(jnp.int32)
    fault_trans = jnp.clip(jnp.exp(math.log(2.0) - 2.9957323 * jax.random.uniform(key_list[9], (NDEV, NFAULT), jnp.float32) ** level_of(key_list[9], (NDEV, NFAULT), ((0, 32),), -0.2, 0.2)), 0.1, 2.0)
    fault_up = set_ends((jax.random.randint(key_list[10], (NDEV, NFAULT), 0, 2) < 1).astype(jnp.int32), jax.random.fold_in(key_list[10], 1), 0, 1)
    cell_owner_keys = jax.random.split(jax.random.fold_in(key_list[11], 1), CELLS // CELLS_DEV)
    cell_owner_turns = jax.random.permutation(jax.random.fold_in(key_list[11], 3), CELLS // CELLS_DEV)
    cell_owner = jax.vmap(lambda own, number: shared_out(jax.random.fold_in(key_list[11], 2), own, number, CELLS_DEV, NDEV, 1, CAPR, 4))(cell_owner_keys, cell_owner_turns).reshape((CELLS, 1))
    return {"pressure": pressure, "mobility": mobility, "mob_deriv": mob_deriv, "accum": accum, "trans": trans, "upwind": upwind, "fault_send": fault_send, "fault_cell": fault_cell, "fault_slot": fault_slot, "fault_trans": fault_trans, "fault_up": fault_up, "cell_owner": cell_owner}


def direction_terms(state_self, state_other, conduct, self_up, count):
    rest = state_self.shape[1:]
    lower = 1.0 - self_up
    diff = state_self[0] - state_other[0]
    mob_up = self_up * state_self[1:count + 1] + lower * state_other[1:count + 1]
    deriv_self = state_self[count + 1:].reshape((count, count) + rest)
    deriv_other = state_other[count + 1:].reshape((count, count) + rest)
    column = (jnp.arange(count) == 0).astype(jnp.float32).reshape((1, count) + (1,) * len(rest))
    pressure_part = mob_up[:, None] * column
    diag_part = conduct * (self_up * diff * deriv_self + pressure_part)
    off_part = conduct * (lower * diff * deriv_other - pressure_part)
    return diag_part, off_part


def to_devices(field):
    lead = field.shape[:-3]
    blocks = field.reshape(lead + (N_TX, GX, N_TY, GY, NZ))
    k = len(lead)
    order = tuple(range(k)) + (k, k + 2, k + 1, k + 3, k + 4)
    return jnp.transpose(blocks, order).reshape(lead + (NDEV, CELLS_DEV))


def reference(pressure, mobility, mob_deriv, accum, trans, upwind, fault_send, fault_cell, fault_slot, fault_trans, fault_up, cell_owner):
    count = NEQ
    nx, ny, nz = pressure.shape
    state = jnp.concatenate([pressure[None], mobility, mob_deriv], 0)
    flags = upwind.astype(jnp.float32)
    widen = ((0, 0), (1, 1), (1, 1), (1, 1))
    wide = jnp.pad(state, widen)
    trans_w = jnp.pad(trans, widen)
    flags_w = jnp.pad(flags, widen)

    def window(field, a, b, c):
        return field[:, a:a + nx, b:b + ny, c:c + nz]

    keep_x = (jnp.arange(nx) < nx - 1).astype(jnp.float32)[:, None, None]
    keep_y = (jnp.arange(ny) < ny - 1).astype(jnp.float32)[None, :, None]
    keep_z = (jnp.arange(nz) < nz - 1).astype(jnp.float32)[None, None, :]
    pairs = [
        (window(wide, 0, 1, 1), window(trans_w, 0, 1, 1)[0], 1.0 - window(flags_w, 0, 1, 1)[0]),
        (window(wide, 2, 1, 1), trans[0] * keep_x, flags[0]),
        (window(wide, 1, 0, 1), window(trans_w, 1, 0, 1)[1], 1.0 - window(flags_w, 1, 0, 1)[1]),
        (window(wide, 1, 2, 1), trans[1] * keep_y, flags[1]),
        (window(wide, 1, 1, 0), window(trans_w, 1, 1, 0)[2], 1.0 - window(flags_w, 1, 1, 0)[2]),
        (window(wide, 1, 1, 2), trans[2] * keep_z, flags[2]),
    ]
    diag = accum.reshape((count, count, nx, ny, nz))
    offs = []
    for other, conduct, self_up in pairs:
        diag_part, off_part = direction_terms(state, other, conduct, self_up, count)
        diag = diag + diag_part
        offs.append(to_devices(off_part))
    diag_dev = to_devices(diag)
    dev_state = to_devices(state)
    source = fault_slot // FCAP
    column = fault_slot % FCAP
    target = jnp.arange(NDEV, dtype=jnp.int32)[:, None] * jnp.ones_like(fault_slot)
    sent_cell = fault_send[source, target, column]
    partner = dev_state[:, source, sent_cell]
    mine = dev_state[:, target, fault_cell]
    fault_diag, fault_off = direction_terms(mine, partner, fault_trans, fault_up.astype(jnp.float32), count)
    diag_dev = diag_dev.at[:, :, target, fault_cell].add(fault_diag)
    fault_block = jnp.zeros((count, count, NDEV, CELLS_DEV), jnp.float32).at[:, :, target, fault_cell].set(fault_off)
    blocks = jnp.stack([diag_dev] + offs + [fault_block], 0).astype(jnp.bfloat16)
    blocks = jnp.pad(blocks, ((0, 0), (0, PAD - count), (0, PAD - count), (0, 0), (0, 0)))
    rows = jnp.transpose(blocks, (3, 4, 0, 1, 2)).reshape(NDEV * CELLS_DEV, 8, PAD * PAD)
    owner = cell_owner[:, 0].reshape(NDEV, CELLS_DEV)
    hits = (owner[:, :, None] == jnp.arange(NDEV, dtype=jnp.int32)[None, None, :]).astype(jnp.int32)
    rank = jnp.sum((jnp.cumsum(hits, 1) - hits) * hits, 2)
    sender = jnp.arange(NDEV, dtype=jnp.int32)[:, None]
    dest = owner * (NDEV * CAPR) + sender * CAPR + rank
    relaid = jnp.zeros((NDEV * NDEV * CAPR, 8, PAD * PAD), jnp.bfloat16).at[dest.reshape(-1)].set(rows)
    return relaid
```

```python
import functools

import jax
import jax.numpy as jnp
from jax import lax
from jax.experimental import pallas as pl
from jax.experimental.pallas import tpu as pltpu
from jax.sharding import PartitionSpec as P

PAD = 16
BLOCKS = 8
LANES = 128
ROWS = 16
MESH = pl.DeviceIdType.MESH
EXACT = lax.Precision.HIGHEST
F32 = jnp.float32
BF16 = jnp.bfloat16
NT = (((1,), (1,)), ((), ()))
TN = (((0,), (0,)), ((), ()))
VMEM_LIMIT = 48 * 1024 * 1024


def iota(shape, dim):
    return lax.broadcasted_iota(jnp.int32, shape, dim)


def build_kernel(
    span_x,
    span_y,
    width,
    count,
    p_ref,
    m_ref,
    deriv_ref,
    acc_ref,
    trans_ref,
    up_ref,
    fsend_ref,
    fcell_ref,
    fslot_ref,
    ftrans_ref,
    fup_ref,
    owner_ref,
    land_off,
    land_diag,
    state_l,
    state_m,
    lower_y_l,
    lower_y_m,
    upper_y_l,
    upper_y_m,
    halo_out,
    halo_in,
    fault_out,
    fault_in,
    send_off,
    send_diag,
    halo_ssem,
    halo_rsem,
    fault_ssem,
    fault_rsem,
    off_ssem,
    off_rsem,
    diag_ssem,
    diag_rsem,
    own_sem,
):
    devices = span_x * span_y
    cells = width * width
    entries = count * count
    shift = width.bit_length() - 1
    lane_p, lane_t, lane_w = entries, entries + 1, entries + 3
    tx = lax.axis_index("tx")
    ty = lax.axis_index("ty")
    me = tx * span_y + ty

    def place(device):
        return (lax.div(device, span_y), lax.rem(device, span_y))

    def partner(step):
        return lax.rem(me + step, devices)

    barrier = pltpu.get_barrier_semaphore()

    def greet(step, carry):
        pl.semaphore_signal(
            barrier, inc=1, device_id=place(partner(step)), device_id_type=MESH
        )
        return carry

    lax.fori_loop(1, devices, greet, 0)

    fields = jnp.concatenate(
        [
            p_ref[...],
            m_ref[...],
            trans_ref[0 : 2 * width, :],
            up_ref[0 : 2 * width, :].astype(F32),
        ],
        0,
    )
    nfield = fields.shape[0]
    spread = ((iota((cells, width), 0) & (width - 1)) == iota((cells, width), 1)).astype(F32)
    crossed = lax.dot_general(spread, fields, NT, precision=EXACT, preferred_element_type=F32)
    same = (iota((cells, nfield), 1) & (width - 1)) == (iota((cells, nfield), 0) >> shift)
    kind = iota((nfield, LANES), 0) >> shift
    lane_of = jnp.where(
        kind == 0,
        lane_p,
        jnp.where(kind <= count, (kind - 1) * count, kind - (count + 1) + lane_t),
    )
    sorter = (iota((nfield, LANES), 1) == lane_of).astype(F32)
    misc = jnp.dot(
        jnp.where(same, crossed, 0.0), sorter, precision=EXACT, preferred_element_type=F32
    )
    state_m[...] = misc
    state_l[...] = jnp.zeros_like(state_l)
    state_l[:, 0:entries] = deriv_ref[...]
    deriv = state_l[...]

    last = cells - width
    halo_out[0, 0:width] = deriv[0:width]
    halo_out[0, width : 2 * width] = misc[0:width]
    halo_out[1, 0:width] = deriv[last:]
    halo_out[1, width : 2 * width] = misc[last:]
    for side, start in ((2, 0), (3, width - 1)):
        halo_out[side, 0:width] = state_l[pl.ds(start, width, stride=width), :]
        halo_out[side, width : 2 * width] = state_m[pl.ds(start, width, stride=width), :]

    ends = (tx > 0, tx < span_x - 1, ty > 0, ty < span_y - 1)
    targets = ((tx - 1, ty), (tx + 1, ty), (tx, ty - 1), (tx, ty + 1))

    def halo_copy(side):
        return pltpu.make_async_remote_copy(
            src_ref=halo_out.at[side],
            dst_ref=halo_in.at[side ^ 1],
            send_sem=halo_ssem.at[side],
            recv_sem=halo_rsem.at[side ^ 1],
            device_id=targets[side],
            device_id_type=MESH,
        )

    def block_copy(src, dst, ssem, rsem, step):
        device = partner(step)
        return pltpu.make_async_remote_copy(
            src_ref=src.at[device],
            dst_ref=dst.at[me],
            send_sem=ssem.at[device],
            recv_sem=rsem.at[me],
            device_id=place(device),
            device_id_type=MESH,
        )

    def block_arrival(src, dst, ssem, rsem, step):
        device = partner(step)
        return pltpu.make_async_remote_copy(
            src_ref=src.at[device],
            dst_ref=dst.at[device],
            send_sem=ssem.at[device],
            recv_sem=rsem.at[device],
            device_id=place(device),
            device_id_type=MESH,
        )

    def each(function):
        def step_body(step, carry):
            function(step)
            return carry

        lax.fori_loop(1, devices, step_body, 0)

    pl.semaphore_wait(barrier, devices - 1)
    for side in range(4):
        pl.when(ends[side])(lambda side=side: halo_copy(side).start())

    caps = fsend_ref.shape[0]
    slab = fault_out.shape[1]
    lines = devices * slab
    slab_shift = slab.bit_length() - 1
    widen = ((iota((devices, lines), 1) >> slab_shift) == iota((devices, lines), 0)).astype(F32)
    picks = jnp.dot(fsend_ref[...].astype(F32), widen, precision=EXACT, preferred_element_type=F32)
    part = iota((1, lines), 1) & (slab - 1)
    index = jnp.where((part & 1) == 0, picks[0:1], picks[1:2])
    hit = iota((cells, lines), 0).astype(F32) == index
    take_l = jnp.where(hit & (part < caps), 1.0, 0.0)
    take_m = jnp.where(hit & (part >= caps) & (part < 2 * caps), 1.0, 0.0)
    gathered = lax.dot_general(
        take_l, deriv, TN, precision=EXACT, preferred_element_type=F32
    ) + lax.dot_general(take_m, misc, TN, precision=EXACT, preferred_element_type=F32)
    fault_out[...] = gathered.reshape(devices, slab, LANES)
    each(lambda step: block_copy(fault_out, fault_in, fault_ssem, fault_rsem, step).start())
    fault_in[pl.ds(me, 1)] = fault_out[pl.ds(me, 1)]

    owner = owner_ref[...]
    named = (iota((devices, cells), 0) == owner).astype(F32)
    before = (iota((cells, cells), 0) < iota((cells, cells), 1)).astype(BF16)
    earlier = jnp.dot(named.astype(BF16), before, preferred_element_type=F32)
    rank = jnp.sum(earlier * named, 0, keepdims=True)
    slot = owner.astype(F32) * ROWS + rank
    slots = devices * ROWS
    mover = jnp.where(iota((slots, cells), 0).astype(F32) == slot, 1.0, 0.0).astype(BF16)

    pressure = misc[:, lane_p : lane_p + 1]
    row = iota((cells, 1), 0)
    at_x = row >> shift
    at_y = row & (width - 1)

    def terms(other_l, other_m, conduct, flag):
        lower = 1.0 - flag
        diff = pressure - other_m[:, lane_p : lane_p + 1]
        mu = conduct * (flag * misc + lower * other_m)
        off = (conduct * lower * diff) * other_l - mu
        return conduct * flag * diff, mu, off

    for side in range(4):
        @pl.when(ends[side])
        def _(side=side):
            halo_copy(side ^ 1).wait_recv()

        @pl.when(jnp.logical_not(ends[side]))
        def _(side=side):
            halo_in[side] = jnp.zeros_like(halo_in[side])

    def column(array, lane):
        return array[:, lane : lane + 1]

    near_l = jnp.concatenate([halo_in[0, 0:width], deriv[:last]], 0)
    near_m = jnp.concatenate([halo_in[0, width : 2 * width], misc[:last]], 0)
    far_l = jnp.concatenate([deriv[width:], halo_in[1, 0:width]], 0)
    far_m = jnp.concatenate([misc[width:], halo_in[1, width : 2 * width]], 0)
    for kept, field, rows, amount, start, side in (
        (lower_y_l, deriv, slice(0, width), 1, 0, 2),
        (lower_y_m, misc, slice(width, 2 * width), 1, 0, 2),
        (upper_y_l, deriv, slice(0, width), cells - 1, width - 1, 3),
        (upper_y_m, misc, slice(width, 2 * width), cells - 1, width - 1, 3),
    ):
        kept[...] = pltpu.roll(field, amount, 0)
        kept[pl.ds(start, width, stride=width), :] = halo_in[side, rows, :]

    keep_x = jnp.where((at_x < width - 1) | (tx < span_x - 1), 1.0, 0.0)
    keep_y = jnp.where((at_y < width - 1) | (ty < span_y - 1), 1.0, 0.0)
    low_y_m = lower_y_m[...]
    sides = (
        (near_l, near_m, column(near_m, lane_t), 1.0 - column(near_m, lane_w)),
        (far_l, far_m, column(misc, lane_t) * keep_x, column(misc, lane_w)),
        (
            lower_y_l[...],
            low_y_m,
            column(low_y_m, lane_t + 1),
            1.0 - column(low_y_m, lane_w + 1),
        ),
        (
            upper_y_l[...],
            upper_y_m[...],
            column(misc, lane_t + 1) * keep_y,
            column(misc, lane_w + 1),
        ),
    )
    scale = jnp.zeros((cells, 1), F32)
    mobile = jnp.zeros((cells, LANES), F32)
    offs = []
    for other_l, other_m, conduct, flag in sides:
        part_scale, mu, off = terms(other_l, other_m, conduct, flag)
        scale = scale + part_scale
        mobile = mobile + mu
        offs.append(off.astype(BF16))

    def send_rows(parts, buffer):
        moved = jnp.dot(
            mover, jnp.concatenate(parts, 1), preferred_element_type=F32
        ).astype(BF16)
        for i in range(len(parts)):
            buffer[:, i * ROWS : (i + 1) * ROWS, :] = moved[
                :, i * LANES : (i + 1) * LANES
            ].reshape(devices, ROWS, LANES)

    send_rows(offs, send_off)
    each(lambda step: block_copy(send_off, land_off, off_ssem, off_rsem, step).start())
    own_off = pltpu.make_async_copy(send_off.at[me], land_off.at[me], own_sem.at[0])
    own_off.start()

    faults = fcell_ref.shape[1]
    chosen = (iota((cells, faults), 0) == fcell_ref[...]).astype(F32)
    fslot = fslot_ref[...]
    line = lax.div(fslot, caps) * slab + lax.rem(fslot, caps)

    def of_cell(values):
        return jnp.sum(chosen * values, 1, keepdims=True)

    base = of_cell(line.astype(F32))
    conduct = of_cell(ftrans_ref[...])
    flag = of_cell(fup_ref[...].astype(F32))
    where = iota((cells, lines), 1).astype(F32)
    pull_l = jnp.where(where == base, 1.0, 0.0)
    pull_m = jnp.where(where == base + caps, 1.0, 0.0)
    each(lambda step: block_arrival(fault_out, fault_in, fault_ssem, fault_rsem, step).wait_recv())
    arrived = fault_in[...].reshape(lines, LANES)
    other_l = jnp.dot(pull_l, arrived, precision=EXACT, preferred_element_type=F32)
    other_m = jnp.dot(pull_m, arrived, precision=EXACT, preferred_element_type=F32)
    part_scale, mu, off = terms(other_l, other_m, conduct, flag)
    diag = (scale + part_scale) * deriv + (mobile + mu)
    state_m[...] = diag
    state_m[:, 0:entries] = state_m[:, 0:entries] + acc_ref[...]
    send_rows([state_m[...].astype(BF16), off.astype(BF16)], send_diag)
    each(lambda step: block_copy(send_diag, land_diag, diag_ssem, diag_rsem, step).start())
    own_diag = pltpu.make_async_copy(send_diag.at[me], land_diag.at[me], own_sem.at[1])
    own_diag.start()

    for side in range(4):
        pl.when(ends[side])(lambda side=side: halo_copy(side).wait_send())
    each(lambda step: block_copy(fault_out, fault_in, fault_ssem, fault_rsem, step).wait_send())
    each(lambda step: block_copy(send_off, land_off, off_ssem, off_rsem, step).wait_send())
    each(lambda step: block_copy(send_diag, land_diag, diag_ssem, diag_rsem, step).wait_send())
    own_off.wait()
    own_diag.wait()
    each(lambda step: block_arrival(send_off, land_off, off_ssem, off_rsem, step).wait_recv())
    each(lambda step: block_arrival(send_diag, land_diag, diag_ssem, diag_rsem, step).wait_recv())


def expand_kernel(capacity, count, off_ref, diag_ref, out_ref):
    group = off_ref.shape[0]
    parts = (off_ref.shape[1] + diag_ref.shape[1]) // ROWS
    tall = capacity * BLOCKS
    part = iota((tall, parts * ROWS), 1) // ROWS
    block = jnp.where(part < 4, part + 1, jnp.where(part == 4, 0, BLOCKS - 1))
    rank = iota((tall, parts * ROWS), 1) % ROWS
    line = iota((tall, parts * ROWS), 0)
    order = ((line // BLOCKS == rank) & (line % BLOCKS == block)).astype(BF16)
    entry = iota((LANES, PAD * PAD), 0)
    target = entry // count * PAD + entry % count
    widen = ((iota((LANES, PAD * PAD), 1) == target) & (entry < count * count)).astype(BF16)
    pieces = []
    for i in range(group):
        lines = jnp.concatenate([off_ref[i], diag_ref[i]], 0)
        pieces.append(jnp.dot(order, lines, preferred_element_type=F32).astype(BF16))
    full = jnp.dot(jnp.concatenate(pieces, 0), widen, preferred_element_type=F32)
    out_ref[...] = full.astype(BF16).reshape(group * capacity, BLOCKS, PAD * PAD)


def body(
    span_x,
    span_y,
    pressure,
    mobility,
    mob_deriv,
    accum,
    trans,
    upwind,
    fault_send,
    fault_cell,
    fault_slot,
    fault_trans,
    fault_up,
    cell_owner,
):
    width = pressure.shape[0]
    count = mobility.shape[0]
    cells = width * width
    devices = span_x * span_y
    capacity = max(2, 2 * cells // devices)
    caps = fault_send.shape[2]
    assert pressure.shape == (width, width, 1) and caps == 2
    entries = count * count
    vmem = pl.BlockSpec(memory_space=pltpu.VMEM)
    anywhere = pl.BlockSpec(memory_space=pl.ANY)
    wide = pltpu.VMEM((cells, LANES), F32)
    sems = pltpu.SemaphoreType.DMA
    land_off, land_diag = pl.pallas_call(
        functools.partial(build_kernel, span_x, span_y, width, count),
        out_shape=(
            jax.ShapeDtypeStruct((devices, 4 * ROWS, LANES), BF16),
            jax.ShapeDtypeStruct((devices, 2 * ROWS, LANES), BF16),
        ),
        in_specs=[vmem] * 12,
        out_specs=(anywhere, anywhere),
        scratch_shapes=[wide] * 6
        + [
            pltpu.VMEM((4, 2 * width, LANES), F32),
            pltpu.VMEM((4, 2 * width, LANES), F32),
            pltpu.VMEM((devices, 8, LANES), F32),
            pltpu.VMEM((devices, 8, LANES), F32),
            pltpu.VMEM((devices, 4 * ROWS, LANES), BF16),
            pltpu.VMEM((devices, 2 * ROWS, LANES), BF16),
            sems((4,)),
            sems((4,)),
            sems((devices,)),
            sems((devices,)),
            sems((devices,)),
            sems((devices,)),
            sems((devices,)),
            sems((devices,)),
            sems((2,)),
        ],
        compiler_params=pltpu.CompilerParams(
            collective_id=0, has_side_effects=True, vmem_limit_bytes=VMEM_LIMIT
        ),
        name="build_rows",
    )(
        pressure.reshape(width, width),
        mobility.reshape(count * width, width),
        jnp.transpose(mob_deriv, (1, 2, 3, 0)).reshape(cells, entries),
        jnp.transpose(accum, (1, 2, 3, 0)).reshape(cells, entries),
        trans.reshape(3 * width, width),
        upwind.reshape(3 * width, width),
        jnp.transpose(fault_send, (0, 2, 1)).reshape(caps, devices),
        fault_cell,
        fault_slot,
        fault_trans,
        fault_up,
        cell_owner.reshape(1, cells),
    )
    group = 8
    return pl.pallas_call(
        functools.partial(expand_kernel, capacity, count),
        grid=(devices // group,),
        out_shape=jax.ShapeDtypeStruct((devices * capacity, BLOCKS, PAD * PAD), BF16),
        in_specs=[
            pl.BlockSpec((group, 4 * ROWS, LANES), lambda i: (i, 0, 0)),
            pl.BlockSpec((group, 2 * ROWS, LANES), lambda i: (i, 0, 0)),
        ],
        out_specs=pl.BlockSpec((group * capacity, BLOCKS, PAD * PAD), lambda i: (i, 0, 0)),
        compiler_params=pltpu.CompilerParams(vmem_limit_bytes=VMEM_LIMIT),
        name="expand_rows",
    )(land_off, land_diag)


def solution(mesh):
    in_specs = (
        P("tx", "ty", None),
        P(None, "tx", "ty", None),
        P(None, "tx", "ty", None),
        P(None, "tx", "ty", None),
        P(None, "tx", "ty", None),
        P(None, "tx", "ty", None),
        P(("tx", "ty"), None, None),
        P(("tx", "ty"), None),
        P(("tx", "ty"), None),
        P(("tx", "ty"), None),
        P(("tx", "ty"), None),
        P(("tx", "ty"), None),
    )
    out_specs = P(("tx", "ty"), None, None)
    local = functools.partial(body, mesh.shape["tx"], mesh.shape["ty"])
    return jax.shard_map(local, mesh=mesh, in_specs=in_specs, out_specs=out_specs, check_vma=False)
```

```python
import functools

import jax
import jax.numpy as jnp
from jax import lax
from jax.experimental import pallas as pl
from jax.experimental.pallas import tpu as pltpu
from jax.sharding import PartitionSpec as P

PAD = 16
BLOCKS = 8
LANES = 128
ROWS = 16
MESH = pl.DeviceIdType.MESH
F32 = jnp.float32
BF16 = jnp.bfloat16
NT = (((1,), (1,)), ((), ()))
VMEM_LIMIT = 60 * 1024 * 1024


def iota(shape, dim):
    return lax.broadcasted_iota(jnp.int32, shape, dim)


def split(values, terms):
    pieces = []
    for _ in range(terms - 1):
        pieces.append(values.astype(BF16))
        values = values - pieces[-1].astype(F32)
    return pieces + [values.astype(BF16)]


def joined(values, terms):
    total = values[:, 0:LANES]
    for i in range(1, terms):
        total = total + values[:, i * LANES : (i + 1) * LANES]
    return total


def one_hot(mask):
    return jnp.where(mask, 1.0, 0.0).astype(BF16)


def build_kernel(
    span_x,
    span_y,
    width,
    count,
    *refs,
):
    sources, refs = refs[:12], refs[12:]
    land_off, land_diag = refs[:2]
    inputs, refs = refs[2:14], refs[14:]
    (
        p_ref,
        m_ref,
        deriv_ref,
        acc_ref,
        trans_ref,
        up_ref,
        fsend_ref,
        fcell_ref,
        fslot_ref,
        ftrans_ref,
        fup_ref,
        owner_ref,
    ) = inputs
    (
        state_l,
        state_m,
        lower_y_l,
        lower_y_m,
        upper_y_l,
        upper_y_m,
        halo_out,
        halo_in,
        fault_out,
        fault_in,
        send_off,
        send_diag,
        input_sem,
        halo_ssem,
        halo_rsem,
        block_ssem,
        block_rsem,
        own_sem,
    ) = refs
    devices = span_x * span_y
    cells = width * width
    entries = count * count
    shift = width.bit_length() - 1
    lane_p, lane_t, lane_w = entries, entries + 1, entries + 3
    tx = lax.axis_index("tx")
    ty = lax.axis_index("ty")
    me = tx * span_y + ty

    loads = [
        pltpu.make_async_copy(source, target, input_sem.at[i])
        for i, (source, target) in enumerate(zip(sources, inputs))
    ]
    for load in loads:
        load.start()

    flips = []
    for code in range(span_y - 1, -1, -1):
        flipped = ty
        for bit in range(span_y.bit_length() - 1):
            if code >> bit & 1:
                flipped = flipped + (1 - 2 * (ty // (1 << bit) % 2)) * (1 << bit)
        flips.append(flipped)

    def each(function):
        def column_of(codes, step):
            x = tx + step
            x = x - jnp.where(x >= span_x, span_x, 0)
            for y in codes:
                function(x, y)

        def run(codes):
            def step_body(step, carry):
                column_of(codes, step)
                return carry

            lax.fori_loop(1, span_x, step_body, 0)

        half = span_y // 2
        column_of(flips[:half], 0)
        run(flips[:half])
        column_of(flips[half : span_y - 1], 0)
        run(flips[half:])

    barrier = pltpu.get_barrier_semaphore()
    each(
        lambda x, y: pl.semaphore_signal(
            barrier, inc=1, device_id=(x, y), device_id_type=MESH
        )
    )

    def send_all(src, dst, kind):
        each(
            lambda x, y: pltpu.make_async_remote_copy(
                src_ref=src.at[x * span_y + y],
                dst_ref=dst.at[me],
                send_sem=block_ssem.at[kind],
                recv_sem=block_rsem.at[kind],
                device_id=(x, y),
                device_id_type=MESH,
            ).start()
        )

    def await_all(buffer, sem):
        span = buffer.at[pl.ds(0, devices - 1)]
        pltpu.make_async_copy(span, span, sem).wait()

    for load in loads:
        load.wait()

    fields = jnp.concatenate(
        [
            p_ref[...],
            m_ref[...],
            trans_ref[0 : 2 * width, :],
            up_ref[0 : 2 * width, :].astype(F32),
        ],
        0,
    )
    nfield = fields.shape[0]
    spread = one_hot((iota((cells, width), 0) & (width - 1)) == iota((cells, width), 1))
    crossed = lax.dot_general(
        jnp.concatenate([spread] * 3, 1),
        jnp.concatenate(split(fields, 3), 1),
        NT,
        preferred_element_type=F32,
    )
    same = (iota((cells, nfield), 1) & (width - 1)) == (iota((cells, nfield), 0) >> shift)
    kind = iota((nfield, LANES), 0) >> shift
    lane_of = jnp.where(
        kind == 0,
        lane_p,
        jnp.where(kind <= count, (kind - 1) * count, kind - (count + 1) + lane_t),
    )
    sorter = one_hot(iota((nfield, LANES), 1) == lane_of)
    misc = jnp.dot(
        jnp.concatenate(split(jnp.where(same, crossed, 0.0), 3), 1),
        jnp.concatenate([sorter] * 3, 0),
        preferred_element_type=F32,
    )
    state_m[...] = misc
    state_l[...] = jnp.zeros_like(state_l)
    state_l[:, 0:entries] = deriv_ref[...]
    deriv = state_l[...]

    last = cells - width
    halo_out[0, 0:width] = deriv[0:width]
    halo_out[0, width : 2 * width] = misc[0:width]
    halo_out[1, 0:width] = deriv[last:]
    halo_out[1, width : 2 * width] = misc[last:]
    for side, start in ((2, 0), (3, width - 1)):
        halo_out[side, 0:width] = state_l[pl.ds(start, width, stride=width), :]
        halo_out[side, width : 2 * width] = state_m[pl.ds(start, width, stride=width), :]

    ends = (tx > 0, tx < span_x - 1, ty > 0, ty < span_y - 1)
    targets = ((tx - 1, ty), (tx + 1, ty), (tx, ty - 1), (tx, ty + 1))

    def halo_copy(side):
        return pltpu.make_async_remote_copy(
            src_ref=halo_out.at[side],
            dst_ref=halo_in.at[side ^ 1],
            send_sem=halo_ssem.at[side],
            recv_sem=halo_rsem.at[side ^ 1],
            device_id=targets[side],
            device_id_type=MESH,
        )

    caps = fsend_ref.shape[0]
    slab = fault_out.shape[1]
    lines = devices * slab
    slab_shift = slab.bit_length() - 1
    widen = one_hot((iota((lines, devices), 0) >> slab_shift) == iota((lines, devices), 1))
    picks = lax.dot_general(
        widen, fsend_ref[...].astype(F32).astype(BF16), NT, preferred_element_type=F32
    )
    part = iota((lines, 1), 0) & (slab - 1)
    index = jnp.where((part & 1) == 0, picks[:, 0:1], picks[:, 1:2])
    hit = iota((lines, cells), 1).astype(F32) == index
    take_l = one_hot(hit & (part < caps))
    take_m = one_hot(hit & (part >= caps) & (part < 2 * caps))
    gathered = joined(
        jnp.dot(take_l, jnp.concatenate(split(deriv, 2), 1), preferred_element_type=F32), 2
    ) + joined(
        jnp.dot(take_m, jnp.concatenate(split(misc, 3), 1), preferred_element_type=F32), 3
    )
    fault_out[...] = gathered.reshape(devices, slab, LANES)
    fault_in[pl.ds(me, 1)] = fault_out[pl.ds(me, 1)]

    pl.semaphore_wait(barrier, devices - 1)
    for side in range(4):
        pl.when(ends[side])(lambda side=side: halo_copy(side).start())
    send_all(fault_out, fault_in, 0)

    owner = owner_ref[...]
    named = (iota((devices, cells), 0) == owner).astype(F32)
    before = one_hot(iota((cells, cells), 0) < iota((cells, cells), 1))
    earlier = jnp.dot(named.astype(BF16), before, preferred_element_type=F32)
    rank = jnp.sum(earlier * named, 0, keepdims=True)
    slot = owner.astype(F32) * ROWS + rank
    slots = devices * ROWS
    mover = one_hot(iota((slots, cells), 0).astype(F32) == slot)

    faults = fcell_ref.shape[1]
    chosen = (iota((cells, faults), 0) == fcell_ref[...]).astype(F32)
    fslot = fslot_ref[...]
    line = lax.div(fslot, caps) * slab + lax.rem(fslot, caps)

    def of_cell(values):
        return jnp.sum(chosen * values, 1, keepdims=True)

    base = of_cell(line.astype(F32))
    fault_conduct = of_cell(ftrans_ref[...])
    fault_flag = of_cell(fup_ref[...].astype(F32))
    where = iota((cells, lines), 1).astype(F32)
    pull_l = one_hot(where == base)
    pull_m = one_hot(where == base + caps)

    pressure = misc[:, lane_p : lane_p + 1]
    row = iota((cells, 1), 0)
    at_x = row >> shift
    at_y = row & (width - 1)

    def terms(other_l, other_m, conduct, flag):
        lower = 1.0 - flag
        diff = pressure - other_m[:, lane_p : lane_p + 1]
        mu = (conduct * flag) * misc + (conduct * lower) * other_m
        off = (conduct * lower * diff) * other_l - mu
        return conduct * flag * diff, mu, off

    for side in range(4):
        @pl.when(ends[side])
        def _(side=side):
            halo_copy(side ^ 1).wait_recv()

        @pl.when(jnp.logical_not(ends[side]))
        def _(side=side):
            halo_in[side] = jnp.zeros_like(halo_in[side])

    def column(array, lane):
        return array[:, lane : lane + 1]

    near_l = jnp.concatenate([halo_in[0, 0:width], deriv[:last]], 0)
    near_m = jnp.concatenate([halo_in[0, width : 2 * width], misc[:last]], 0)
    far_l = jnp.concatenate([deriv[width:], halo_in[1, 0:width]], 0)
    far_m = jnp.concatenate([misc[width:], halo_in[1, width : 2 * width]], 0)
    for kept, field, rows, amount, start, side in (
        (lower_y_l, deriv, slice(0, width), 1, 0, 2),
        (lower_y_m, misc, slice(width, 2 * width), 1, 0, 2),
        (upper_y_l, deriv, slice(0, width), cells - 1, width - 1, 3),
        (upper_y_m, misc, slice(width, 2 * width), cells - 1, width - 1, 3),
    ):
        kept[...] = pltpu.roll(field, amount, 0)
        kept[pl.ds(start, width, stride=width), :] = halo_in[side, rows, :]

    keep_x = jnp.where((at_x < width - 1) | (tx < span_x - 1), 1.0, 0.0)
    keep_y = jnp.where((at_y < width - 1) | (ty < span_y - 1), 1.0, 0.0)
    low_y_m = lower_y_m[...]
    sides = (
        (near_l, near_m, column(near_m, lane_t), 1.0 - column(near_m, lane_w)),
        (far_l, far_m, column(misc, lane_t) * keep_x, column(misc, lane_w)),
        (
            lower_y_l[...],
            low_y_m,
            column(low_y_m, lane_t + 1),
            1.0 - column(low_y_m, lane_w + 1),
        ),
        (
            upper_y_l[...],
            upper_y_m[...],
            column(misc, lane_t + 1) * keep_y,
            column(misc, lane_w + 1),
        ),
    )
    scale = jnp.zeros((cells, 1), F32)
    mobile = jnp.zeros((cells, LANES), F32)
    offs = []
    for other_l, other_m, conduct, flag in sides:
        part_scale, mu, off = terms(other_l, other_m, conduct, flag)
        scale = scale + part_scale
        mobile = mobile + mu
        offs.append(off.astype(BF16))

    def place_rows(parts, buffer):
        moved = jnp.dot(
            mover, jnp.concatenate(parts, 1), preferred_element_type=F32
        ).astype(BF16)
        for i in range(len(parts)):
            buffer[:, i * ROWS : (i + 1) * ROWS, :] = moved[
                :, i * LANES : (i + 1) * LANES
            ].reshape(devices, ROWS, LANES)

    place_rows(offs, send_off)
    send_all(send_off, land_off, 1)
    own_off = pltpu.make_async_copy(send_off.at[me], land_off.at[me], own_sem.at[0])
    own_off.start()

    await_all(fault_in, block_rsem.at[0])
    arrived = fault_in[...].reshape(lines, LANES)
    pieces = split(arrived, 3)
    other_l = joined(
        jnp.dot(pull_l, jnp.concatenate(pieces[:2], 1), preferred_element_type=F32), 2
    )
    other_m = joined(
        jnp.dot(pull_m, jnp.concatenate(pieces, 1), preferred_element_type=F32), 3
    )
    part_scale, mu, off = terms(other_l, other_m, fault_conduct, fault_flag)
    diag = (scale + part_scale) * deriv + (mobile + mu)
    state_m[...] = diag
    state_m[:, 0:entries] = state_m[:, 0:entries] + acc_ref[...]
    place_rows([state_m[...].astype(BF16), off.astype(BF16)], send_diag)
    send_all(send_diag, land_diag, 2)
    own_diag = pltpu.make_async_copy(send_diag.at[me], land_diag.at[me], own_sem.at[1])
    own_diag.start()

    for side in range(4):
        pl.when(ends[side])(lambda side=side: halo_copy(side).wait_send())
    await_all(fault_out, block_ssem.at[0])
    await_all(send_off, block_ssem.at[1])
    await_all(send_diag, block_ssem.at[2])
    own_off.wait()
    own_diag.wait()
    await_all(land_off, block_rsem.at[1])
    await_all(land_diag, block_rsem.at[2])


def expand_kernel(capacity, count, off_ref, diag_ref, out_ref, wide_ref):
    group = off_ref.shape[0]
    tall = capacity * BLOCKS
    entry = iota((LANES, PAD * PAD), 0)
    target = entry // count * PAD + entry % count
    widen = one_hot((iota((LANES, PAD * PAD), 1) == target) & (entry < count * count))
    for ref, blocks in ((off_ref, (1, 2, 3, 4)), (diag_ref, (0, BLOCKS - 1))):
        lines = ref[...].reshape(group * len(blocks) * ROWS, LANES)
        full = jnp.dot(lines, widen, preferred_element_type=F32)
        for i in range(group):
            for j, block in enumerate(blocks):
                start = (i * len(blocks) + j) * ROWS
                for half in range(2):
                    wide_ref[half, pl.ds(i * tall + block, capacity, stride=BLOCKS), :] = full[
                        start : start + capacity, half * LANES : (half + 1) * LANES
                    ]
    gap = jnp.zeros((group * capacity, LANES), F32)
    for block in (5, 6):
        for half in range(2):
            wide_ref[half, pl.ds(block, group * capacity, stride=BLOCKS), :] = gap
    for half in range(2):
        out_ref[:, :, half * LANES : (half + 1) * LANES] = (
            wide_ref[half].astype(BF16).reshape(group * capacity, BLOCKS, LANES)
        )


def body(
    span_x,
    span_y,
    pressure,
    mobility,
    mob_deriv,
    accum,
    trans,
    upwind,
    fault_send,
    fault_cell,
    fault_slot,
    fault_trans,
    fault_up,
    cell_owner,
):
    width = pressure.shape[0]
    count = mobility.shape[0]
    cells = width * width
    devices = span_x * span_y
    capacity = max(2, 2 * cells // devices)
    caps = fault_send.shape[2]
    assert pressure.shape == (width, width, 1) and caps == 2
    entries = count * count
    anywhere = pl.BlockSpec(memory_space=pl.ANY)
    wide = pltpu.VMEM((cells, LANES), F32)
    sems = pltpu.SemaphoreType.DMA
    arrays = (
        pressure.reshape(width, width),
        mobility.reshape(count * width, width),
        jnp.transpose(mob_deriv, (1, 2, 3, 0)).reshape(cells, entries),
        jnp.transpose(accum, (1, 2, 3, 0)).reshape(cells, entries),
        trans.reshape(3 * width, width),
        upwind.reshape(3 * width, width),
        jnp.transpose(fault_send, (0, 2, 1)).reshape(caps, devices),
        fault_cell,
        fault_slot,
        fault_trans,
        fault_up,
        cell_owner.reshape(1, cells),
    )
    land_off, land_diag = pl.pallas_call(
        functools.partial(build_kernel, span_x, span_y, width, count),
        out_shape=(
            jax.ShapeDtypeStruct((devices, 4 * ROWS, LANES), BF16),
            jax.ShapeDtypeStruct((devices, 2 * ROWS, LANES), BF16),
        ),
        in_specs=[pl.BlockSpec(memory_space=pltpu.HBM)] * 12,
        out_specs=(anywhere, anywhere),
        scratch_shapes=[pltpu.VMEM(array.shape, array.dtype) for array in arrays]
        + [wide] * 6
        + [
            pltpu.VMEM((4, 2 * width, LANES), F32),
            pltpu.VMEM((4, 2 * width, LANES), F32),
            pltpu.VMEM((devices, 8, LANES), F32),
            pltpu.VMEM((devices, 8, LANES), F32),
            pltpu.VMEM((devices, 4 * ROWS, LANES), BF16),
            pltpu.VMEM((devices, 2 * ROWS, LANES), BF16),
            sems((len(arrays),)),
            sems((4,)),
            sems((4,)),
            sems((3,)),
            sems((3,)),
            sems((2,)),
        ],
        compiler_params=pltpu.CompilerParams(
            collective_id=0, has_side_effects=True, vmem_limit_bytes=VMEM_LIMIT
        ),
        name="build_rows",
    )(*arrays)
    group = 8
    return pl.pallas_call(
        functools.partial(expand_kernel, capacity, count),
        grid=(devices // group,),
        out_shape=jax.ShapeDtypeStruct((devices * capacity, BLOCKS, PAD * PAD), BF16),
        in_specs=[
            pl.BlockSpec((group, 4 * ROWS, LANES), lambda i: (i, 0, 0)),
            pl.BlockSpec((group, 2 * ROWS, LANES), lambda i: (i, 0, 0)),
        ],
        out_specs=pl.BlockSpec((group * capacity, BLOCKS, PAD * PAD), lambda i: (i, 0, 0)),
        scratch_shapes=[pltpu.VMEM((2, group * capacity * BLOCKS, LANES), F32)],
        compiler_params=pltpu.CompilerParams(vmem_limit_bytes=VMEM_LIMIT),
        name="expand_rows",
    )(land_off, land_diag)


def solution(mesh):
    in_specs = (
        P("tx", "ty", None),
        P(None, "tx", "ty", None),
        P(None, "tx", "ty", None),
        P(None, "tx", "ty", None),
        P(None, "tx", "ty", None),
        P(None, "tx", "ty", None),
        P(("tx", "ty"), None, None),
        P(("tx", "ty"), None),
        P(("tx", "ty"), None),
        P(("tx", "ty"), None),
        P(("tx", "ty"), None),
        P(("tx", "ty"), None),
    )
    out_specs = P(("tx", "ty"), None, None)
    local = functools.partial(body, mesh.shape["tx"], mesh.shape["ty"])
    return jax.shard_map(local, mesh=mesh, in_specs=in_specs, out_specs=out_specs, check_vma=False)
```

```python
import functools

import jax
import jax.numpy as jnp
from jax import lax
from jax.experimental import pallas as pl
from jax.experimental.pallas import tpu as pltpu
from jax.sharding import PartitionSpec as P

PAD = 16
BLOCKS = 8
LANES = 128
ROWS = 16
MESH = pl.DeviceIdType.MESH
F32 = jnp.float32
BF16 = jnp.bfloat16
NT = (((1,), (1,)), ((), ()))
VMEM_LIMIT = 60 * 1024 * 1024


def iota(shape, dim):
    return lax.broadcasted_iota(jnp.int32, shape, dim)


def split(values, terms):
    pieces = []
    for _ in range(terms - 1):
        pieces.append(values.astype(BF16))
        values = values - pieces[-1].astype(F32)
    return pieces + [values.astype(BF16)]


def joined(values, terms):
    total = values[:, 0:LANES]
    for i in range(1, terms):
        total = total + values[:, i * LANES : (i + 1) * LANES]
    return total


def one_hot(mask):
    return jnp.where(mask, 1.0, 0.0).astype(BF16)


def build_kernel(
    span_x,
    span_y,
    width,
    count,
    *refs,
):
    sources, refs = refs[:12], refs[12:]
    land_off, land_diag = refs[:2]
    inputs, refs = refs[2:14], refs[14:]
    (
        p_ref,
        m_ref,
        deriv_ref,
        acc_ref,
        trans_ref,
        up_ref,
        fsend_ref,
        fcell_ref,
        fslot_ref,
        ftrans_ref,
        fup_ref,
        owner_ref,
    ) = inputs
    (
        state_l,
        state_m,
        lower_y_l,
        lower_y_m,
        upper_y_l,
        upper_y_m,
        halo_out,
        halo_in,
        fault_out,
        fault_in,
        send_off,
        send_diag,
        input_sem,
        halo_ssem,
        halo_rsem,
        block_ssem,
        block_rsem,
        own_sem,
    ) = refs
    devices = span_x * span_y
    cells = width * width
    entries = count * count
    shift = width.bit_length() - 1
    lane_p, lane_t, lane_w = entries, entries + 1, entries + 3
    tx = lax.axis_index("tx")
    ty = lax.axis_index("ty")
    me = tx * span_y + ty

    loads = [
        pltpu.make_async_copy(source, target, input_sem.at[i])
        for i, (source, target) in enumerate(zip(sources, inputs))
    ]
    for load in loads:
        load.start()

    flips = []
    for code in range(span_y - 1, -1, -1):
        flipped = ty
        for bit in range(span_y.bit_length() - 1):
            if code >> bit & 1:
                flipped = flipped + (1 - 2 * (ty // (1 << bit) % 2)) * (1 << bit)
        flips.append(flipped)

    def each(function):
        def column_of(codes, step):
            x = tx + step
            x = x - jnp.where(x >= span_x, span_x, 0)
            for y in codes:
                function(x, y)

        def run(codes):
            def step_body(step, carry):
                column_of(codes, step)
                return carry

            lax.fori_loop(1, span_x, step_body, 0)

        half = span_y // 2
        column_of(flips[:half], 0)
        run(flips[:half])
        column_of(flips[half : span_y - 1], 0)
        run(flips[half:])

    barrier = pltpu.get_barrier_semaphore()
    each(
        lambda x, y: pl.semaphore_signal(
            barrier, inc=1, device_id=(x, y), device_id_type=MESH
        )
    )

    def send_all(src, dst, kind):
        each(
            lambda x, y: pltpu.make_async_remote_copy(
                src_ref=src.at[x * span_y + y],
                dst_ref=dst.at[me],
                send_sem=block_ssem.at[kind],
                recv_sem=block_rsem.at[kind],
                device_id=(x, y),
                device_id_type=MESH,
            ).start()
        )

    def await_all(buffer, sem):
        span = buffer.at[pl.ds(0, devices - 1)]
        pltpu.make_async_copy(span, span, sem).wait()

    for load in loads:
        load.wait()

    fields = jnp.concatenate(
        [
            p_ref[...],
            m_ref[...],
            trans_ref[0 : 2 * width, :],
            up_ref[0 : 2 * width, :].astype(F32),
        ],
        0,
    )
    nfield = fields.shape[0]
    spread = one_hot((iota((cells, width), 0) & (width - 1)) == iota((cells, width), 1))
    crossed = lax.dot_general(
        jnp.concatenate([spread] * 3, 1),
        jnp.concatenate(split(fields, 3), 1),
        NT,
        preferred_element_type=F32,
    )
    same = (iota((cells, nfield), 1) & (width - 1)) == (iota((cells, nfield), 0) >> shift)
    kind = iota((nfield, LANES), 0) >> shift
    lane_of = jnp.where(
        kind == 0,
        lane_p,
        jnp.where(kind <= count, (kind - 1) * count, kind - (count + 1) + lane_t),
    )
    sorter = one_hot(iota((nfield, LANES), 1) == lane_of)
    misc = jnp.dot(
        jnp.concatenate(split(jnp.where(same, crossed, 0.0), 3), 1),
        jnp.concatenate([sorter] * 3, 0),
        preferred_element_type=F32,
    )
    state_m[...] = misc
    state_l[...] = jnp.zeros_like(state_l)
    state_l[:, 0:entries] = deriv_ref[...]
    deriv = state_l[...]

    last = cells - width
    halo_out[0, 0:width] = deriv[0:width]
    halo_out[0, width : 2 * width] = misc[0:width]
    halo_out[1, 0:width] = deriv[last:]
    halo_out[1, width : 2 * width] = misc[last:]
    for side, start in ((2, 0), (3, width - 1)):
        halo_out[side, 0:width] = state_l[pl.ds(start, width, stride=width), :]
        halo_out[side, width : 2 * width] = state_m[pl.ds(start, width, stride=width), :]

    ends = (tx > 0, tx < span_x - 1, ty > 0, ty < span_y - 1)
    targets = ((tx - 1, ty), (tx + 1, ty), (tx, ty - 1), (tx, ty + 1))

    def halo_copy(side):
        return pltpu.make_async_remote_copy(
            src_ref=halo_out.at[side],
            dst_ref=halo_in.at[side ^ 1],
            send_sem=halo_ssem.at[side],
            recv_sem=halo_rsem.at[side ^ 1],
            device_id=targets[side],
            device_id_type=MESH,
        )

    pl.semaphore_wait(barrier, devices - 1)
    for side in range(4):
        pl.when(ends[side])(lambda side=side: halo_copy(side).start())

    caps = fsend_ref.shape[0]
    slab = fault_out.shape[1]
    lines = devices * slab
    slab_shift = slab.bit_length() - 1
    widen = one_hot((iota((lines, devices), 0) >> slab_shift) == iota((lines, devices), 1))
    picks = lax.dot_general(
        widen, fsend_ref[...].astype(F32).astype(BF16), NT, preferred_element_type=F32
    )
    part = iota((lines, 1), 0) & (slab - 1)
    index = jnp.where((part & 1) == 0, picks[:, 0:1], picks[:, 1:2])
    hit = iota((lines, cells), 1).astype(F32) == index
    take_l = one_hot(hit & (part < caps))
    take_m = one_hot(hit & (part >= caps))
    gathered = joined(
        jnp.dot(take_l, jnp.concatenate(split(deriv, 2), 1), preferred_element_type=F32), 2
    ) + joined(
        jnp.dot(take_m, jnp.concatenate(split(misc, 3), 1), preferred_element_type=F32), 3
    )
    fault_out[...] = gathered.reshape(devices, slab, LANES)
    fault_in[pl.ds(me, 1)] = fault_out[pl.ds(me, 1)]

    send_all(fault_out, fault_in, 0)

    owner = owner_ref[...]
    named = (iota((devices, cells), 0) == owner).astype(F32)
    before = one_hot(iota((cells, cells), 0) < iota((cells, cells), 1))
    earlier = jnp.dot(named.astype(BF16), before, preferred_element_type=F32)
    rank = jnp.sum(earlier * named, 0, keepdims=True)
    slot = owner.astype(F32) * ROWS + rank
    slots = devices * ROWS
    mover = one_hot(iota((slots, cells), 0).astype(F32) == slot)

    faults = fcell_ref.shape[1]
    chosen = (iota((cells, faults), 0) == fcell_ref[...]).astype(F32)
    fslot = fslot_ref[...]
    line = lax.div(fslot, caps) * slab + lax.rem(fslot, caps)

    def of_cell(values):
        return jnp.sum(chosen * values, 1, keepdims=True)

    base = of_cell(line.astype(F32))
    fault_conduct = of_cell(ftrans_ref[...])
    fault_flag = of_cell(fup_ref[...].astype(F32))
    where = iota((cells, lines), 1).astype(F32)
    pull_l = one_hot(where == base)
    pull_m = one_hot(where == base + caps)

    pressure = misc[:, lane_p : lane_p + 1]
    row = iota((cells, 1), 0)
    at_x = row >> shift
    at_y = row & (width - 1)

    def terms(other_l, other_m, conduct, flag):
        lower = 1.0 - flag
        diff = pressure - other_m[:, lane_p : lane_p + 1]
        mu = (conduct * flag) * misc + (conduct * lower) * other_m
        off = (conduct * lower * diff) * other_l - mu
        return conduct * flag * diff, mu, off

    for side in range(4):
        @pl.when(ends[side])
        def _(side=side):
            halo_copy(side ^ 1).wait_recv()

        @pl.when(jnp.logical_not(ends[side]))
        def _(side=side):
            halo_in[side] = jnp.zeros_like(halo_in[side])

    def column(array, lane):
        return array[:, lane : lane + 1]

    near_l = jnp.concatenate([halo_in[0, 0:width], deriv[:last]], 0)
    near_m = jnp.concatenate([halo_in[0, width : 2 * width], misc[:last]], 0)
    far_l = jnp.concatenate([deriv[width:], halo_in[1, 0:width]], 0)
    far_m = jnp.concatenate([misc[width:], halo_in[1, width : 2 * width]], 0)
    for kept, field, rows, amount, start, side in (
        (lower_y_l, deriv, slice(0, width), 1, 0, 2),
        (lower_y_m, misc, slice(width, 2 * width), 1, 0, 2),
        (upper_y_l, deriv, slice(0, width), cells - 1, width - 1, 3),
        (upper_y_m, misc, slice(width, 2 * width), cells - 1, width - 1, 3),
    ):
        kept[...] = pltpu.roll(field, amount, 0)
        kept[pl.ds(start, width, stride=width), :] = halo_in[side, rows, :]

    keep_x = jnp.where((at_x < width - 1) | (tx < span_x - 1), 1.0, 0.0)
    keep_y = jnp.where((at_y < width - 1) | (ty < span_y - 1), 1.0, 0.0)
    low_y_m = lower_y_m[...]
    sides = (
        (near_l, near_m, column(near_m, lane_t), 1.0 - column(near_m, lane_w)),
        (far_l, far_m, column(misc, lane_t) * keep_x, column(misc, lane_w)),
        (
            lower_y_l[...],
            low_y_m,
            column(low_y_m, lane_t + 1),
            1.0 - column(low_y_m, lane_w + 1),
        ),
        (
            upper_y_l[...],
            upper_y_m[...],
            column(misc, lane_t + 1) * keep_y,
            column(misc, lane_w + 1),
        ),
    )
    scale = jnp.zeros((cells, 1), F32)
    mobile = jnp.zeros((cells, LANES), F32)
    offs = []
    for other_l, other_m, conduct, flag in sides:
        part_scale, mu, off = terms(other_l, other_m, conduct, flag)
        scale = scale + part_scale
        mobile = mobile + mu
        offs.append(off.astype(BF16))

    def place_rows(parts, buffer):
        moved = jnp.dot(
            mover, jnp.concatenate(parts, 1), preferred_element_type=F32
        ).astype(BF16)
        for i in range(len(parts)):
            buffer[:, i * ROWS : (i + 1) * ROWS, :] = moved[
                :, i * LANES : (i + 1) * LANES
            ].reshape(devices, ROWS, LANES)

    place_rows(offs, send_off)
    send_all(send_off, land_off, 1)
    own_off = pltpu.make_async_copy(send_off.at[me], land_off.at[me], own_sem.at[0])
    own_off.start()

    await_all(fault_in, block_rsem.at[0])
    arrived = fault_in[...].reshape(lines, LANES)
    pieces = split(arrived, 3)
    other_l = joined(
        jnp.dot(pull_l, jnp.concatenate(pieces[:2], 1), preferred_element_type=F32), 2
    )
    other_m = joined(
        jnp.dot(pull_m, jnp.concatenate(pieces, 1), preferred_element_type=F32), 3
    )
    part_scale, mu, off = terms(other_l, other_m, fault_conduct, fault_flag)
    diag = (scale + part_scale) * deriv + (mobile + mu)
    state_m[...] = diag
    state_m[:, 0:entries] = state_m[:, 0:entries] + acc_ref[...]
    place_rows([state_m[...].astype(BF16), off.astype(BF16)], send_diag)
    send_all(send_diag, land_diag, 2)
    own_diag = pltpu.make_async_copy(send_diag.at[me], land_diag.at[me], own_sem.at[1])
    own_diag.start()

    for side in range(4):
        pl.when(ends[side])(lambda side=side: halo_copy(side).wait_send())
    await_all(fault_out, block_ssem.at[0])
    await_all(send_off, block_ssem.at[1])
    await_all(send_diag, block_ssem.at[2])
    own_off.wait()
    own_diag.wait()
    await_all(land_off, block_rsem.at[1])
    await_all(land_diag, block_rsem.at[2])


def expand_kernel(capacity, count, group, off_hbm, diag_hbm, out_hbm, off_ref, diag_ref, out_ref, in_sem, out_sem):
    devices = off_hbm.shape[0]
    pieces = devices // group
    fetches = []
    for i in range(pieces):
        part = pl.ds(i * group, group)
        fetches.append(
            (
                pltpu.make_async_copy(off_hbm.at[part], off_ref.at[part], in_sem.at[0, i]),
                pltpu.make_async_copy(diag_hbm.at[part], diag_ref.at[part], in_sem.at[1, i]),
            )
        )
        for fetch in fetches[-1]:
            fetch.start()
    kinds = (off_ref.shape[1] + diag_ref.shape[1]) // ROWS
    tall = capacity * BLOCKS
    kind = iota((tall, kinds * ROWS), 1) // ROWS
    block = jnp.where(kind < 4, kind + 1, jnp.where(kind == 4, 0, BLOCKS - 1))
    rank = iota((tall, kinds * ROWS), 1) % ROWS
    line = iota((tall, kinds * ROWS), 0)
    order = one_hot((line // BLOCKS == rank) & (line % BLOCKS == block))
    entry = iota((LANES, PAD * PAD), 0)
    target = entry // count * PAD + entry % count
    widen = one_hot((iota((LANES, PAD * PAD), 1) == target) & (entry < count * count))
    stores = []
    for i in range(pieces):
        for fetch in fetches[i]:
            fetch.wait()
        ordered = []
        for j in range(i * group, (i + 1) * group, 2):
            pair = jnp.concatenate(
                [
                    jnp.concatenate([off_ref[j], off_ref[j + 1]], 1),
                    jnp.concatenate([diag_ref[j], diag_ref[j + 1]], 1),
                ],
                0,
            )
            both = jnp.dot(order, pair, preferred_element_type=F32).astype(BF16)
            ordered += [both[:, :LANES], both[:, LANES:]]
        full = jnp.dot(jnp.concatenate(ordered, 0), widen, preferred_element_type=F32)
        rows = pl.ds(i * group * capacity, group * capacity)
        out_ref[rows] = full.astype(BF16).reshape(group * capacity, BLOCKS, PAD * PAD)
        stores.append(pltpu.make_async_copy(out_ref.at[rows], out_hbm.at[rows], out_sem.at[i]))
        stores[-1].start()
    for store in stores:
        store.wait()


def body(
    span_x,
    span_y,
    pressure,
    mobility,
    mob_deriv,
    accum,
    trans,
    upwind,
    fault_send,
    fault_cell,
    fault_slot,
    fault_trans,
    fault_up,
    cell_owner,
):
    width = pressure.shape[0]
    count = mobility.shape[0]
    cells = width * width
    devices = span_x * span_y
    capacity = max(2, 2 * cells // devices)
    caps = fault_send.shape[2]
    assert pressure.shape == (width, width, 1) and caps == 2
    entries = count * count
    anywhere = pl.BlockSpec(memory_space=pl.ANY)
    wide = pltpu.VMEM((cells, LANES), F32)
    sems = pltpu.SemaphoreType.DMA
    arrays = (
        pressure.reshape(width, width),
        mobility.reshape(count * width, width),
        jnp.transpose(mob_deriv, (1, 2, 3, 0)).reshape(cells, entries),
        jnp.transpose(accum, (1, 2, 3, 0)).reshape(cells, entries),
        trans.reshape(3 * width, width),
        upwind.reshape(3 * width, width),
        jnp.transpose(fault_send, (0, 2, 1)).reshape(caps, devices),
        fault_cell,
        fault_slot,
        fault_trans,
        fault_up,
        cell_owner.reshape(1, cells),
    )
    land_off, land_diag = pl.pallas_call(
        functools.partial(build_kernel, span_x, span_y, width, count),
        out_shape=(
            jax.ShapeDtypeStruct((devices, 4 * ROWS, LANES), BF16),
            jax.ShapeDtypeStruct((devices, 2 * ROWS, LANES), BF16),
        ),
        in_specs=[pl.BlockSpec(memory_space=pltpu.HBM)] * 12,
        out_specs=(anywhere, anywhere),
        scratch_shapes=[pltpu.VMEM(array.shape, array.dtype) for array in arrays]
        + [wide] * 6
        + [
            pltpu.VMEM((4, 2 * width, LANES), F32),
            pltpu.VMEM((4, 2 * width, LANES), F32),
            pltpu.VMEM((devices, 2 * caps, LANES), F32),
            pltpu.VMEM((devices, 2 * caps, LANES), F32),
            pltpu.VMEM((devices, 4 * ROWS, LANES), BF16),
            pltpu.VMEM((devices, 2 * ROWS, LANES), BF16),
            sems((len(arrays),)),
            sems((4,)),
            sems((4,)),
            sems((3,)),
            sems((3,)),
            sems((2,)),
        ],
        compiler_params=pltpu.CompilerParams(
            collective_id=0, has_side_effects=True, vmem_limit_bytes=VMEM_LIMIT
        ),
        name="build_rows",
    )(*arrays)
    group = devices // 8
    full = (devices * capacity, BLOCKS, PAD * PAD)
    return pl.pallas_call(
        functools.partial(expand_kernel, capacity, count, group),
        out_shape=jax.ShapeDtypeStruct(full, BF16),
        in_specs=[anywhere] * 2,
        out_specs=anywhere,
        scratch_shapes=[
            pltpu.VMEM(land_off.shape, BF16),
            pltpu.VMEM(land_diag.shape, BF16),
            pltpu.VMEM(full, BF16),
            sems((2, devices // group)),
            sems((devices // group,)),
        ],
        compiler_params=pltpu.CompilerParams(vmem_limit_bytes=VMEM_LIMIT),
        name="expand_rows",
    )(land_off, land_diag)


def solution(mesh):
    in_specs = (
        P("tx", "ty", None),
        P(None, "tx", "ty", None),
        P(None, "tx", "ty", None),
        P(None, "tx", "ty", None),
        P(None, "tx", "ty", None),
        P(None, "tx", "ty", None),
        P(("tx", "ty"), None, None),
        P(("tx", "ty"), None),
        P(("tx", "ty"), None),
        P(("tx", "ty"), None),
        P(("tx", "ty"), None),
        P(("tx", "ty"), None),
    )
    out_specs = P(("tx", "ty"), None, None)
    local = functools.partial(body, mesh.shape["tx"], mesh.shape["ty"])
    return jax.shard_map(local, mesh=mesh, in_specs=in_specs, out_specs=out_specs, check_vma=False)
```

```python
import functools

import jax
import jax.numpy as jnp
from jax import lax
from jax.experimental import pallas as pl
from jax.experimental.pallas import tpu as pltpu
from jax.sharding import PartitionSpec as P

PAD = 16
BLOCKS = 8
LANES = 128
ROWS = 16
MESH = pl.DeviceIdType.MESH
F32 = jnp.float32
BF16 = jnp.bfloat16
NT = (((1,), (1,)), ((), ()))
VMEM_LIMIT = 60 * 1024 * 1024


def iota(shape, dim):
    return lax.broadcasted_iota(jnp.int32, shape, dim)


def split(values, terms):
    pieces = []
    for _ in range(terms - 1):
        pieces.append(values.astype(BF16))
        values = values - pieces[-1].astype(F32)
    return pieces + [values.astype(BF16)]


def joined(values, terms):
    total = values[:, 0:LANES]
    for i in range(1, terms):
        total = total + values[:, i * LANES : (i + 1) * LANES]
    return total


def one_hot(mask):
    return jnp.where(mask, 1.0, 0.0).astype(BF16)


def build_kernel(
    span_x,
    span_y,
    width,
    count,
    *refs,
):
    sources, out_hbm, inputs, refs = refs[:12], refs[12], refs[13:25], refs[25:]
    (
        p_ref,
        m_ref,
        deriv_ref,
        acc_ref,
        trans_ref,
        up_ref,
        fsend_ref,
        fcell_ref,
        fslot_ref,
        ftrans_ref,
        fup_ref,
        owner_ref,
    ) = inputs
    (
        state_l,
        state_m,
        lower_y_l,
        lower_y_m,
        upper_y_l,
        upper_y_m,
        halo_out,
        halo_in,
        fault_out,
        fault_in,
        send_off,
        send_diag,
        land_off,
        land_diag,
        order_ref,
        widen_ref,
        out_ref,
        input_sem,
        halo_ssem,
        halo_rsem,
        block_ssem,
        fault_rsem,
        off_rsem,
        diag_rsem,
        out_sem,
    ) = refs
    devices = span_x * span_y
    cells = width * width
    entries = count * count
    shift = width.bit_length() - 1
    lane_p, lane_t, lane_w = entries, entries + 1, entries + 3
    tx = lax.axis_index("tx")
    ty = lax.axis_index("ty")
    me = tx * span_y + ty

    loads = [
        pltpu.make_async_copy(source, target, input_sem.at[i])
        for i, (source, target) in enumerate(zip(sources, inputs))
    ]
    for load in loads:
        load.start()

    flips = []
    for code in range(span_y - 1, -1, -1):
        flipped = ty
        for bit in range(span_y.bit_length() - 1):
            if code >> bit & 1:
                flipped = flipped + (1 - 2 * (ty // (1 << bit) % 2)) * (1 << bit)
        flips.append(flipped)

    half = span_y // 2
    across, near = flips[:half], flips[half:]

    def column_of(function, codes, step):
        x = tx + step
        x = x - jnp.where(x >= span_x, span_x, 0)
        for y in codes:
            function(x, y)

    def columns_of(function, codes, first):
        def step_body(step, carry):
            column_of(function, codes, step)
            return carry

        lax.fori_loop(first, span_x, step_body, 0)

    def each_across(function):
        columns_of(function, across, 0)

    def each_near(function):
        column_of(function, near[:-1], 0)
        columns_of(function, near, 1)

    def each(function):
        each_across(function)
        each_near(function)

    barrier = pltpu.get_barrier_semaphore()
    each(
        lambda x, y: pl.semaphore_signal(
            barrier, inc=1, device_id=(x, y), device_id_type=MESH
        )
    )

    def sender(src, dst, kind, rsem):
        return lambda x, y: pltpu.make_async_remote_copy(
            src_ref=src.at[x * span_y + y],
            dst_ref=dst.at[me],
            send_sem=block_ssem.at[kind],
            recv_sem=rsem,
            device_id=(x, y),
            device_id_type=MESH,
        ).start()

    def await_all(buffer, sem):
        span = buffer.at[pl.ds(0, devices - 1)]
        pltpu.make_async_copy(span, span, sem).wait()

    for load in loads:
        load.wait()

    fields = jnp.concatenate(
        [
            p_ref[...],
            m_ref[...],
            trans_ref[0 : 2 * width, :],
            up_ref[0 : 2 * width, :].astype(F32),
        ],
        0,
    )
    nfield = fields.shape[0]
    spread = one_hot((iota((cells, width), 0) & (width - 1)) == iota((cells, width), 1))
    crossed = lax.dot_general(
        jnp.concatenate([spread] * 3, 1),
        jnp.concatenate(split(fields, 3), 1),
        NT,
        preferred_element_type=F32,
    )
    same = (iota((cells, nfield), 1) & (width - 1)) == (iota((cells, nfield), 0) >> shift)
    kind = iota((nfield, LANES), 0) >> shift
    lane_of = jnp.where(
        kind == 0,
        lane_p,
        jnp.where(kind <= count, (kind - 1) * count, kind - (count + 1) + lane_t),
    )
    sorter = one_hot(iota((nfield, LANES), 1) == lane_of)
    misc = jnp.dot(
        jnp.concatenate(split(jnp.where(same, crossed, 0.0), 3), 1),
        jnp.concatenate([sorter] * 3, 0),
        preferred_element_type=F32,
    )
    state_m[...] = misc
    state_l[...] = jnp.zeros_like(state_l)
    state_l[:, 0:entries] = deriv_ref[...]
    deriv = state_l[...]

    last = cells - width
    halo_out[0, 0:width] = deriv[0:width]
    halo_out[0, width : 2 * width] = misc[0:width]
    halo_out[1, 0:width] = deriv[last:]
    halo_out[1, width : 2 * width] = misc[last:]
    for side, start in ((2, 0), (3, width - 1)):
        halo_out[side, 0:width] = state_l[pl.ds(start, width, stride=width), :]
        halo_out[side, width : 2 * width] = state_m[pl.ds(start, width, stride=width), :]

    ends = (tx > 0, tx < span_x - 1, ty > 0, ty < span_y - 1)
    targets = ((tx - 1, ty), (tx + 1, ty), (tx, ty - 1), (tx, ty + 1))

    def halo_copy(side):
        return pltpu.make_async_remote_copy(
            src_ref=halo_out.at[side],
            dst_ref=halo_in.at[side ^ 1],
            send_sem=halo_ssem.at[side],
            recv_sem=halo_rsem.at[side ^ 1],
            device_id=targets[side],
            device_id_type=MESH,
        )

    pl.semaphore_wait(barrier, devices - 1)
    for side in range(4):
        pl.when(ends[side])(lambda side=side: halo_copy(side).start())

    caps = fsend_ref.shape[0]
    slab = fault_out.shape[1]
    lines = devices * slab
    slab_shift = slab.bit_length() - 1
    widen = one_hot((iota((lines, devices), 0) >> slab_shift) == iota((lines, devices), 1))
    picks = lax.dot_general(
        widen, fsend_ref[...].astype(F32).astype(BF16), NT, preferred_element_type=F32
    )
    part = iota((lines, 1), 0) & (slab - 1)
    index = jnp.where((part & 1) == 0, picks[:, 0:1], picks[:, 1:2])
    hit = iota((lines, cells), 1).astype(F32) == index
    take_l = one_hot(hit & (part < caps))
    take_m = one_hot(hit & (part >= caps))
    gathered = joined(
        jnp.dot(take_l, jnp.concatenate(split(deriv, 2), 1), preferred_element_type=F32), 2
    ) + joined(
        jnp.dot(take_m, jnp.concatenate(split(misc, 3), 1), preferred_element_type=F32), 3
    )
    fault_out[...] = gathered.reshape(devices, slab, LANES)
    fault_in[pl.ds(me, 1)] = fault_out[pl.ds(me, 1)]

    each(sender(fault_out, fault_in, 0, fault_rsem.at[0]))

    owner = owner_ref[...]
    named = (iota((devices, cells), 0) == owner).astype(F32)
    before = one_hot(iota((cells, cells), 0) < iota((cells, cells), 1))
    earlier = jnp.dot(named.astype(BF16), before, preferred_element_type=F32)
    rank = jnp.sum(earlier * named, 0, keepdims=True)
    slot = owner.astype(F32) * ROWS + rank
    slots = devices * ROWS
    mover = one_hot(iota((slots, cells), 0).astype(F32) == slot)

    faults = fcell_ref.shape[1]
    chosen = (iota((cells, faults), 0) == fcell_ref[...]).astype(F32)
    fslot = fslot_ref[...]
    line = lax.div(fslot, caps) * slab + lax.rem(fslot, caps)

    def of_cell(values):
        return jnp.sum(chosen * values, 1, keepdims=True)

    base = of_cell(line.astype(F32))
    fault_conduct = of_cell(ftrans_ref[...])
    fault_flag = of_cell(fup_ref[...].astype(F32))
    where = iota((cells, lines), 1).astype(F32)
    pull_l = one_hot(where == base)
    pull_m = one_hot(where == base + caps)

    pressure = misc[:, lane_p : lane_p + 1]
    row = iota((cells, 1), 0)
    at_x = row >> shift
    at_y = row & (width - 1)

    def terms(other_l, other_m, conduct, flag):
        lower = 1.0 - flag
        diff = pressure - other_m[:, lane_p : lane_p + 1]
        mu = (conduct * flag) * misc + (conduct * lower) * other_m
        off = (conduct * lower * diff) * other_l - mu
        return conduct * flag * diff, mu, off

    for side in range(4):
        @pl.when(ends[side])
        def _(side=side):
            halo_copy(side ^ 1).wait_recv()

        @pl.when(jnp.logical_not(ends[side]))
        def _(side=side):
            halo_in[side] = jnp.zeros_like(halo_in[side])

    def column(array, lane):
        return array[:, lane : lane + 1]

    near_l = jnp.concatenate([halo_in[0, 0:width], deriv[:last]], 0)
    near_m = jnp.concatenate([halo_in[0, width : 2 * width], misc[:last]], 0)
    far_l = jnp.concatenate([deriv[width:], halo_in[1, 0:width]], 0)
    far_m = jnp.concatenate([misc[width:], halo_in[1, width : 2 * width]], 0)
    for kept, field, rows, amount, start, side in (
        (lower_y_l, deriv, slice(0, width), 1, 0, 2),
        (lower_y_m, misc, slice(width, 2 * width), 1, 0, 2),
        (upper_y_l, deriv, slice(0, width), cells - 1, width - 1, 3),
        (upper_y_m, misc, slice(width, 2 * width), cells - 1, width - 1, 3),
    ):
        kept[...] = pltpu.roll(field, amount, 0)
        kept[pl.ds(start, width, stride=width), :] = halo_in[side, rows, :]

    keep_x = jnp.where((at_x < width - 1) | (tx < span_x - 1), 1.0, 0.0)
    keep_y = jnp.where((at_y < width - 1) | (ty < span_y - 1), 1.0, 0.0)
    low_y_m = lower_y_m[...]
    sides = (
        (near_l, near_m, column(near_m, lane_t), 1.0 - column(near_m, lane_w)),
        (far_l, far_m, column(misc, lane_t) * keep_x, column(misc, lane_w)),
        (
            lower_y_l[...],
            low_y_m,
            column(low_y_m, lane_t + 1),
            1.0 - column(low_y_m, lane_w + 1),
        ),
        (
            upper_y_l[...],
            upper_y_m[...],
            column(misc, lane_t + 1) * keep_y,
            column(misc, lane_w + 1),
        ),
    )
    scale = jnp.zeros((cells, 1), F32)
    mobile = jnp.zeros((cells, LANES), F32)
    offs = []
    for other_l, other_m, conduct, flag in sides:
        part_scale, mu, off = terms(other_l, other_m, conduct, flag)
        scale = scale + part_scale
        mobile = mobile + mu
        offs.append(off.astype(BF16))

    def place_rows(parts, buffer):
        moved = jnp.dot(
            mover, jnp.concatenate(parts, 1), preferred_element_type=F32
        ).astype(BF16)
        for i in range(len(parts)):
            buffer[:, i * ROWS : (i + 1) * ROWS, :] = moved[
                :, i * LANES : (i + 1) * LANES
            ].reshape(devices, ROWS, LANES)

    place_rows(offs, send_off)
    each(sender(send_off, land_off, 1, off_rsem.at[me]))
    land_off[pl.ds(me, 1)] = send_off[pl.ds(me, 1)]

    capacity = out_ref.shape[0] // devices
    shape = order_ref.shape
    kind = iota(shape, 1) // ROWS
    block = jnp.where(kind < 4, kind + 1, jnp.where(kind == 4, 0, BLOCKS - 1))
    line_to = iota(shape, 0)
    order_ref[...] = one_hot(
        (line_to // BLOCKS == iota(shape, 1) % ROWS) & (line_to % BLOCKS == block)
    )
    shape = widen_ref.shape
    entry = iota(shape, 0)
    target = entry // count * PAD + entry % count
    widen_ref[...] = one_hot((iota(shape, 1) == target) & (entry < entries))

    await_all(fault_in, fault_rsem.at[0])
    arrived = fault_in[...].reshape(lines, LANES)
    pieces = split(arrived, 3)
    other_l = joined(
        jnp.dot(pull_l, jnp.concatenate(pieces[:2], 1), preferred_element_type=F32), 2
    )
    other_m = joined(
        jnp.dot(pull_m, jnp.concatenate(pieces, 1), preferred_element_type=F32), 3
    )
    part_scale, mu, off = terms(other_l, other_m, fault_conduct, fault_flag)
    diag = (scale + part_scale) * deriv + (mobile + mu)
    state_m[...] = diag
    state_m[:, 0:entries] = state_m[:, 0:entries] + acc_ref[...]
    place_rows([state_m[...].astype(BF16), off.astype(BF16)], send_diag)
    each_near(sender(send_diag, land_diag, 2, diag_rsem.at[me]))
    each_across(sender(send_diag, land_diag, 2, diag_rsem.at[me]))
    land_diag[pl.ds(me, 1)] = send_diag[pl.ds(me, 1)]

    def arrive(x, y):
        source = x * span_y + y
        for land, sem in ((land_off, off_rsem), (land_diag, diag_rsem)):
            pltpu.make_async_copy(land.at[source], land.at[source], sem.at[source]).wait()

    def expand(x, first, second):
        pair = [x * span_y + first, x * span_y + second]
        lines = jnp.concatenate(
            [
                jnp.concatenate([land[source] for source in pair], 1)
                for land in (land_off, land_diag)
            ],
            0,
        )
        both = jnp.dot(order_ref[...], lines, preferred_element_type=F32).astype(BF16)
        for source, ordered in zip(pair, (both[:, :LANES], both[:, LANES:])):
            full = jnp.dot(ordered, widen_ref[...], preferred_element_type=F32)
            rows = pl.ds(source * capacity, capacity)
            out_ref[rows] = full.astype(BF16).reshape(capacity, BLOCKS, PAD * PAD)
            pltpu.make_async_copy(out_ref.at[rows], out_hbm.at[rows], out_sem.at[0]).start()

    def finish(codes, first):
        def step_body(step, carry):
            column_of(arrive, codes, step)
            x = tx + step
            x = x - jnp.where(x >= span_x, span_x, 0)
            for i in range(0, len(codes), 2):
                expand(x, codes[i], codes[i + 1])
            return carry

        lax.fori_loop(first, span_x, step_body, 0)

    column_of(arrive, near[:-1], 0)
    for i in range(0, half, 2):
        expand(tx, near[i], near[i + 1])
    finish(near, 1)
    finish(across, 0)

    for side in range(4):
        pl.when(ends[side])(lambda side=side: halo_copy(side).wait_send())
    await_all(fault_out, block_ssem.at[0])
    await_all(send_off, block_ssem.at[1])
    await_all(send_diag, block_ssem.at[2])
    pltpu.make_async_copy(out_ref, out_hbm, out_sem.at[0]).wait()


def body(
    span_x,
    span_y,
    pressure,
    mobility,
    mob_deriv,
    accum,
    trans,
    upwind,
    fault_send,
    fault_cell,
    fault_slot,
    fault_trans,
    fault_up,
    cell_owner,
):
    width = pressure.shape[0]
    count = mobility.shape[0]
    cells = width * width
    devices = span_x * span_y
    capacity = max(2, 2 * cells // devices)
    caps = fault_send.shape[2]
    assert pressure.shape == (width, width, 1) and caps == 2
    entries = count * count
    anywhere = pl.BlockSpec(memory_space=pl.ANY)
    wide = pltpu.VMEM((cells, LANES), F32)
    sems = pltpu.SemaphoreType.DMA
    arrays = (
        pressure.reshape(width, width),
        mobility.reshape(count * width, width),
        jnp.transpose(mob_deriv, (1, 2, 3, 0)).reshape(cells, entries),
        jnp.transpose(accum, (1, 2, 3, 0)).reshape(cells, entries),
        trans.reshape(3 * width, width),
        upwind.reshape(3 * width, width),
        jnp.transpose(fault_send, (0, 2, 1)).reshape(caps, devices),
        fault_cell,
        fault_slot,
        fault_trans,
        fault_up,
        cell_owner.reshape(1, cells),
    )
    full = (devices * capacity, BLOCKS, PAD * PAD)
    return pl.pallas_call(
        functools.partial(build_kernel, span_x, span_y, width, count),
        out_shape=jax.ShapeDtypeStruct(full, BF16),
        in_specs=[pl.BlockSpec(memory_space=pltpu.HBM)] * 12,
        out_specs=anywhere,
        scratch_shapes=[pltpu.VMEM(array.shape, array.dtype) for array in arrays]
        + [wide] * 6
        + [
            pltpu.VMEM((4, 2 * width, LANES), F32),
            pltpu.VMEM((4, 2 * width, LANES), F32),
            pltpu.VMEM((devices, 2 * caps, LANES), F32),
            pltpu.VMEM((devices, 2 * caps, LANES), F32),
            pltpu.VMEM((devices, 4 * ROWS, LANES), BF16),
            pltpu.VMEM((devices, 2 * ROWS, LANES), BF16),
            pltpu.VMEM((devices, 4 * ROWS, LANES), BF16),
            pltpu.VMEM((devices, 2 * ROWS, LANES), BF16),
            pltpu.VMEM((capacity * BLOCKS, 6 * ROWS), BF16),
            pltpu.VMEM((LANES, PAD * PAD), BF16),
            pltpu.VMEM(full, BF16),
            sems((len(arrays),)),
            sems((4,)),
            sems((4,)),
            sems((3,)),
            sems((1,)),
            sems((devices,)),
            sems((devices,)),
            sems((1,)),
        ],
        compiler_params=pltpu.CompilerParams(
            collective_id=0, has_side_effects=True, vmem_limit_bytes=VMEM_LIMIT
        ),
        name="build_rows",
    )(*arrays)


def solution(mesh):
    in_specs = (
        P("tx", "ty", None),
        P(None, "tx", "ty", None),
        P(None, "tx", "ty", None),
        P(None, "tx", "ty", None),
        P(None, "tx", "ty", None),
        P(None, "tx", "ty", None),
        P(("tx", "ty"), None, None),
        P(("tx", "ty"), None),
        P(("tx", "ty"), None),
        P(("tx", "ty"), None),
        P(("tx", "ty"), None),
        P(("tx", "ty"), None),
    )
    out_specs = P(("tx", "ty"), None, None)
    local = functools.partial(body, mesh.shape["tx"], mesh.shape["ty"])
    return jax.shard_map(local, mesh=mesh, in_specs=in_specs, out_specs=out_specs, check_vma=False)
```

```python
import functools

import jax
import jax.numpy as jnp
from jax import lax
from jax.experimental import pallas as pl
from jax.experimental.pallas import tpu as pltpu
from jax.sharding import PartitionSpec as P

PAD = 16
BLOCKS = 8
LANES = 128
ROWS = 16
MESH = pl.DeviceIdType.MESH
F32 = jnp.float32
BF16 = jnp.bfloat16
NT = (((1,), (1,)), ((), ()))
VMEM_LIMIT = 48 * 1024 * 1024
EXPAND_LIMIT = 32 * 1024 * 1024


def iota(shape, dim):
    return lax.broadcasted_iota(jnp.int32, shape, dim)


def split(values, terms):
    pieces = []
    for _ in range(terms - 1):
        pieces.append(values.astype(BF16))
        values = values - pieces[-1].astype(F32)
    return pieces + [values.astype(BF16)]


def joined(values, terms):
    total = values[:, 0:LANES]
    for i in range(1, terms):
        total = total + values[:, i * LANES : (i + 1) * LANES]
    return total


def one_hot(mask):
    return jnp.where(mask, 1.0, 0.0).astype(BF16)


def build_kernel(
    span_x,
    span_y,
    width,
    count,
    *refs,
):
    sources, refs = refs[:12], refs[12:]
    land_off, land_diag = refs[:2]
    inputs, refs = refs[2:14], refs[14:]
    (
        p_ref,
        m_ref,
        deriv_ref,
        acc_ref,
        trans_ref,
        up_ref,
        fsend_ref,
        fcell_ref,
        fslot_ref,
        ftrans_ref,
        fup_ref,
        owner_ref,
    ) = inputs
    (
        state_l,
        state_m,
        lower_y_l,
        lower_y_m,
        upper_y_l,
        upper_y_m,
        halo_out,
        halo_in,
        fault_out,
        fault_in,
        send_off,
        send_diag,
        input_sem,
        halo_ssem,
        halo_rsem,
        block_ssem,
        block_rsem,
        own_sem,
    ) = refs
    devices = span_x * span_y
    cells = width * width
    entries = count * count
    shift = width.bit_length() - 1
    lane_p, lane_t, lane_w = entries, entries + 1, entries + 3
    tx = lax.axis_index("tx")
    ty = lax.axis_index("ty")
    me = tx * span_y + ty

    loads = [
        pltpu.make_async_copy(source, target, input_sem.at[i])
        for i, (source, target) in enumerate(zip(sources, inputs))
    ]
    for load in loads:
        load.start()

    flips = []
    for code in range(span_y - 1, -1, -1):
        flipped = ty
        for bit in range(span_y.bit_length() - 1):
            if code >> bit & 1:
                flipped = flipped + (1 - 2 * (ty // (1 << bit) % 2)) * (1 << bit)
        flips.append(flipped)

    def each(function):
        def column_of(codes, step):
            x = tx + step
            x = x - jnp.where(x >= span_x, span_x, 0)
            for y in codes:
                function(x, y)

        def run(codes):
            def step_body(step, carry):
                column_of(codes, step)
                return carry

            lax.fori_loop(1, span_x, step_body, 0)

        half = span_y // 2
        column_of(flips[:half], 0)
        run(flips[:half])
        column_of(flips[half : span_y - 1], 0)
        run(flips[half:])

    barrier = pltpu.get_barrier_semaphore()
    each(
        lambda x, y: pl.semaphore_signal(
            barrier, inc=1, device_id=(x, y), device_id_type=MESH
        )
    )

    def send_all(src, dst, kind):
        each(
            lambda x, y: pltpu.make_async_remote_copy(
                src_ref=src.at[x * span_y + y],
                dst_ref=dst.at[me],
                send_sem=block_ssem.at[kind],
                recv_sem=block_rsem.at[kind],
                device_id=(x, y),
                device_id_type=MESH,
            ).start()
        )

    def await_all(buffer, sem):
        span = buffer.at[pl.ds(0, devices - 1)]
        pltpu.make_async_copy(span, span, sem).wait()

    for load in loads:
        load.wait()

    fields = jnp.concatenate(
        [
            p_ref[...],
            m_ref[...],
            trans_ref[0 : 2 * width, :],
            up_ref[0 : 2 * width, :].astype(F32),
        ],
        0,
    )
    nfield = fields.shape[0]
    spread = one_hot((iota((cells, width), 0) & (width - 1)) == iota((cells, width), 1))
    crossed = lax.dot_general(
        jnp.concatenate([spread] * 3, 1),
        jnp.concatenate(split(fields, 3), 1),
        NT,
        preferred_element_type=F32,
    )
    same = (iota((cells, nfield), 1) & (width - 1)) == (iota((cells, nfield), 0) >> shift)
    kind = iota((nfield, LANES), 0) >> shift
    lane_of = jnp.where(
        kind == 0,
        lane_p,
        jnp.where(kind <= count, (kind - 1) * count, kind - (count + 1) + lane_t),
    )
    sorter = one_hot(iota((nfield, LANES), 1) == lane_of)
    misc = jnp.dot(
        jnp.concatenate(split(jnp.where(same, crossed, 0.0), 3), 1),
        jnp.concatenate([sorter] * 3, 0),
        preferred_element_type=F32,
    )
    state_m[...] = misc
    state_l[...] = jnp.zeros_like(state_l)
    state_l[:, 0:entries] = deriv_ref[...]
    deriv = state_l[...]

    last = cells - width
    halo_out[0, 0:width] = deriv[0:width]
    halo_out[0, width : 2 * width] = misc[0:width]
    halo_out[1, 0:width] = deriv[last:]
    halo_out[1, width : 2 * width] = misc[last:]
    for side, start in ((2, 0), (3, width - 1)):
        halo_out[side, 0:width] = state_l[pl.ds(start, width, stride=width), :]
        halo_out[side, width : 2 * width] = state_m[pl.ds(start, width, stride=width), :]

    ends = (tx > 0, tx < span_x - 1, ty > 0, ty < span_y - 1)
    targets = ((tx - 1, ty), (tx + 1, ty), (tx, ty - 1), (tx, ty + 1))

    def halo_copy(side):
        return pltpu.make_async_remote_copy(
            src_ref=halo_out.at[side],
            dst_ref=halo_in.at[side ^ 1],
            send_sem=halo_ssem.at[side],
            recv_sem=halo_rsem.at[side ^ 1],
            device_id=targets[side],
            device_id_type=MESH,
        )

    caps = fsend_ref.shape[0]
    slab = fault_out.shape[1]
    lines = devices * slab
    slab_shift = slab.bit_length() - 1
    widen = one_hot((iota((lines, devices), 0) >> slab_shift) == iota((lines, devices), 1))
    picks = lax.dot_general(
        widen, fsend_ref[...].astype(F32).astype(BF16), NT, preferred_element_type=F32
    )
    part = iota((lines, 1), 0) & (slab - 1)
    index = jnp.where((part & 1) == 0, picks[:, 0:1], picks[:, 1:2])
    hit = iota((lines, cells), 1).astype(F32) == index
    take_l = one_hot(hit & (part < caps))
    take_m = one_hot(hit & (part >= caps))
    gathered = joined(
        jnp.dot(take_l, jnp.concatenate(split(deriv, 2), 1), preferred_element_type=F32), 2
    ) + joined(
        jnp.dot(take_m, jnp.concatenate(split(misc, 3), 1), preferred_element_type=F32), 3
    )
    fault_out[...] = gathered.reshape(devices, slab, LANES)
    fault_in[pl.ds(me, 1)] = fault_out[pl.ds(me, 1)]


    owner = owner_ref[...]
    named = (iota((devices, cells), 0) == owner).astype(F32)
    before = one_hot(iota((cells, cells), 0) < iota((cells, cells), 1))
    earlier = jnp.dot(named.astype(BF16), before, preferred_element_type=F32)
    rank = jnp.sum(earlier * named, 0, keepdims=True)
    slot = owner.astype(F32) * ROWS + rank
    slots = devices * ROWS
    mover = one_hot(iota((slots, cells), 0).astype(F32) == slot)

    faults = fcell_ref.shape[1]
    chosen = (iota((cells, faults), 0) == fcell_ref[...]).astype(F32)
    fslot = fslot_ref[...]
    line = lax.div(fslot, caps) * slab + lax.rem(fslot, caps)

    def of_cell(values):
        return jnp.sum(chosen * values, 1, keepdims=True)

    base = of_cell(line.astype(F32))
    fault_conduct = of_cell(ftrans_ref[...])
    fault_flag = of_cell(fup_ref[...].astype(F32))
    where = iota((cells, lines), 1).astype(F32)
    pull_l = one_hot(where == base)
    pull_m = one_hot(where == base + caps)

    pl.semaphore_wait(barrier, devices - 1)
    for side in range(4):
        pl.when(ends[side])(lambda side=side: halo_copy(side).start())
    send_all(fault_out, fault_in, 0)

    pressure = misc[:, lane_p : lane_p + 1]
    row = iota((cells, 1), 0)
    at_x = row >> shift
    at_y = row & (width - 1)

    def terms(other_l, other_m, conduct, flag):
        lower = 1.0 - flag
        diff = pressure - other_m[:, lane_p : lane_p + 1]
        mu = (conduct * flag) * misc + (conduct * lower) * other_m
        off = (conduct * lower * diff) * other_l - mu
        return conduct * flag * diff, mu, off

    for side in range(4):
        @pl.when(ends[side])
        def _(side=side):
            halo_copy(side ^ 1).wait_recv()

        @pl.when(jnp.logical_not(ends[side]))
        def _(side=side):
            halo_in[side] = jnp.zeros_like(halo_in[side])

    def column(array, lane):
        return array[:, lane : lane + 1]

    near_l = jnp.concatenate([halo_in[0, 0:width], deriv[:last]], 0)
    near_m = jnp.concatenate([halo_in[0, width : 2 * width], misc[:last]], 0)
    far_l = jnp.concatenate([deriv[width:], halo_in[1, 0:width]], 0)
    far_m = jnp.concatenate([misc[width:], halo_in[1, width : 2 * width]], 0)
    for kept, field, rows, amount, start, side in (
        (lower_y_l, deriv, slice(0, width), 1, 0, 2),
        (lower_y_m, misc, slice(width, 2 * width), 1, 0, 2),
        (upper_y_l, deriv, slice(0, width), cells - 1, width - 1, 3),
        (upper_y_m, misc, slice(width, 2 * width), cells - 1, width - 1, 3),
    ):
        kept[...] = pltpu.roll(field, amount, 0)
        kept[pl.ds(start, width, stride=width), :] = halo_in[side, rows, :]

    keep_x = jnp.where((at_x < width - 1) | (tx < span_x - 1), 1.0, 0.0)
    keep_y = jnp.where((at_y < width - 1) | (ty < span_y - 1), 1.0, 0.0)
    low_y_m = lower_y_m[...]
    sides = (
        (near_l, near_m, column(near_m, lane_t), 1.0 - column(near_m, lane_w)),
        (far_l, far_m, column(misc, lane_t) * keep_x, column(misc, lane_w)),
        (
            lower_y_l[...],
            low_y_m,
            column(low_y_m, lane_t + 1),
            1.0 - column(low_y_m, lane_w + 1),
        ),
        (
            upper_y_l[...],
            upper_y_m[...],
            column(misc, lane_t + 1) * keep_y,
            column(misc, lane_w + 1),
        ),
    )
    scale = jnp.zeros((cells, 1), F32)
    mobile = jnp.zeros((cells, LANES), F32)
    offs = []
    for other_l, other_m, conduct, flag in sides:
        part_scale, mu, off = terms(other_l, other_m, conduct, flag)
        scale = scale + part_scale
        mobile = mobile + mu
        offs.append(off.astype(BF16))

    def place_rows(parts, buffer):
        moved = jnp.dot(
            mover, jnp.concatenate(parts, 1), preferred_element_type=F32
        ).astype(BF16)
        for i in range(len(parts)):
            buffer[:, i * ROWS : (i + 1) * ROWS, :] = moved[
                :, i * LANES : (i + 1) * LANES
            ].reshape(devices, ROWS, LANES)

    place_rows(offs, send_off)
    send_all(send_off, land_off, 1)
    own_off = pltpu.make_async_copy(send_off.at[me], land_off.at[me], own_sem.at[0])
    own_off.start()

    await_all(fault_in, block_rsem.at[0])
    arrived = fault_in[...].reshape(lines, LANES)
    pieces = split(arrived, 3)
    other_l = joined(
        jnp.dot(pull_l, jnp.concatenate(pieces[:2], 1), preferred_element_type=F32), 2
    )
    other_m = joined(
        jnp.dot(pull_m, jnp.concatenate(pieces, 1), preferred_element_type=F32), 3
    )
    part_scale, mu, off = terms(other_l, other_m, fault_conduct, fault_flag)
    diag = (scale + part_scale) * deriv + (mobile + mu)
    state_m[...] = diag
    state_m[:, 0:entries] = state_m[:, 0:entries] + acc_ref[...]
    place_rows([state_m[...].astype(BF16), off.astype(BF16)], send_diag)
    send_all(send_diag, land_diag, 2)
    own_diag = pltpu.make_async_copy(send_diag.at[me], land_diag.at[me], own_sem.at[1])
    own_diag.start()

    for side in range(4):
        pl.when(ends[side])(lambda side=side: halo_copy(side).wait_send())
    await_all(fault_out, block_ssem.at[0])
    await_all(send_off, block_ssem.at[1])
    await_all(send_diag, block_ssem.at[2])
    own_off.wait()
    own_diag.wait()
    await_all(land_off, block_rsem.at[1])
    await_all(land_diag, block_rsem.at[2])


def expand_kernel(capacity, count, group, off_ref, diag_ref, out_ref):
    kinds = (off_ref.shape[1] + diag_ref.shape[1]) // ROWS
    tall = capacity * BLOCKS
    kind = iota((tall, kinds * ROWS), 1) // ROWS
    block = jnp.where(kind < 4, kind + 1, jnp.where(kind == 4, 0, BLOCKS - 1))
    rank = iota((tall, kinds * ROWS), 1) % ROWS
    line = iota((tall, kinds * ROWS), 0)
    order = one_hot((line // BLOCKS == rank) & (line % BLOCKS == block))
    entry = iota((LANES, PAD * PAD), 0)
    target = entry // count * PAD + entry % count
    widen = one_hot((iota((LANES, PAD * PAD), 1) == target) & (entry < count * count))
    first = pl.program_id(0) * group
    ordered = []
    for i in range(0, group, 2):
        pair = jnp.concatenate(
            [
                jnp.concatenate([land[first + i], land[first + i + 1]], 1)
                for land in (off_ref, diag_ref)
            ],
            0,
        )
        both = jnp.dot(order, pair, preferred_element_type=F32).astype(BF16)
        ordered += [both[:, :LANES], both[:, LANES:]]
    full = jnp.dot(jnp.concatenate(ordered, 0), widen, preferred_element_type=F32)
    out_ref[...] = full.astype(BF16).reshape(group * capacity, BLOCKS, PAD * PAD)


def body(
    span_x,
    span_y,
    pressure,
    mobility,
    mob_deriv,
    accum,
    trans,
    upwind,
    fault_send,
    fault_cell,
    fault_slot,
    fault_trans,
    fault_up,
    cell_owner,
):
    width = pressure.shape[0]
    count = mobility.shape[0]
    cells = width * width
    devices = span_x * span_y
    capacity = max(2, 2 * cells // devices)
    caps = fault_send.shape[2]
    assert pressure.shape == (width, width, 1) and caps == 2
    entries = count * count
    vmem = pl.BlockSpec(memory_space=pltpu.VMEM)
    wide = pltpu.VMEM((cells, LANES), F32)
    sems = pltpu.SemaphoreType.DMA
    arrays = (
        pressure.reshape(width, width),
        mobility.reshape(count * width, width),
        jnp.transpose(mob_deriv, (1, 2, 3, 0)).reshape(cells, entries),
        jnp.transpose(accum, (1, 2, 3, 0)).reshape(cells, entries),
        trans.reshape(3 * width, width),
        upwind.reshape(3 * width, width),
        jnp.transpose(fault_send, (0, 2, 1)).reshape(caps, devices),
        fault_cell,
        fault_slot,
        fault_trans,
        fault_up,
        cell_owner.reshape(1, cells),
    )
    land_off, land_diag = pl.pallas_call(
        functools.partial(build_kernel, span_x, span_y, width, count),
        out_shape=(
            pltpu.VMEM((devices, 4 * ROWS, LANES), BF16),
            pltpu.VMEM((devices, 2 * ROWS, LANES), BF16),
        ),
        in_specs=[pl.BlockSpec(memory_space=pltpu.HBM)] * 12,
        out_specs=(vmem, vmem),
        scratch_shapes=[pltpu.VMEM(array.shape, array.dtype) for array in arrays]
        + [wide] * 6
        + [
            pltpu.VMEM((4, 2 * width, LANES), F32),
            pltpu.VMEM((4, 2 * width, LANES), F32),
            pltpu.VMEM((devices, 2 * caps, LANES), F32),
            pltpu.VMEM((devices, 2 * caps, LANES), F32),
            pltpu.VMEM((devices, 4 * ROWS, LANES), BF16),
            pltpu.VMEM((devices, 2 * ROWS, LANES), BF16),
            sems((len(arrays),)),
            sems((4,)),
            sems((4,)),
            sems((3,)),
            sems((3,)),
            sems((2,)),
        ],
        compiler_params=pltpu.CompilerParams(
            collective_id=0, has_side_effects=True, vmem_limit_bytes=VMEM_LIMIT
        ),
        name="build_rows",
    )(*[pltpu.with_memory_space_constraint(array, pltpu.HBM) for array in arrays])
    group = devices // 4
    full = (devices * capacity, BLOCKS, PAD * PAD)
    return pl.pallas_call(
        functools.partial(expand_kernel, capacity, count, group),
        grid=(devices // group,),
        out_shape=jax.ShapeDtypeStruct(full, BF16),
        in_specs=[vmem] * 2,
        out_specs=pl.BlockSpec((group * capacity,) + full[1:], lambda i: (i, 0, 0)),
        compiler_params=pltpu.CompilerParams(vmem_limit_bytes=EXPAND_LIMIT),
        name="expand_rows",
    )(land_off, land_diag)


def solution(mesh):
    in_specs = (
        P("tx", "ty", None),
        P(None, "tx", "ty", None),
        P(None, "tx", "ty", None),
        P(None, "tx", "ty", None),
        P(None, "tx", "ty", None),
        P(None, "tx", "ty", None),
        P(("tx", "ty"), None, None),
        P(("tx", "ty"), None),
        P(("tx", "ty"), None),
        P(("tx", "ty"), None),
        P(("tx", "ty"), None),
        P(("tx", "ty"), None),
    )
    out_specs = P(("tx", "ty"), None, None)
    local = functools.partial(body, mesh.shape["tx"], mesh.shape["ty"])
    return jax.shard_map(local, mesh=mesh, in_specs=in_specs, out_specs=out_specs, check_vma=False)
```

```python
import functools

import jax
import jax.numpy as jnp
from jax import lax
from jax.experimental import pallas as pl
from jax.experimental.pallas import tpu as pltpu
from jax.sharding import PartitionSpec as P

PAD = 16
BLOCKS = 8
LANES = 128
ROWS = 16
MESH = pl.DeviceIdType.MESH
F32 = jnp.float32
BF16 = jnp.bfloat16
NT = (((1,), (1,)), ((), ()))
VMEM_LIMIT = 48 * 1024 * 1024
EXPAND_LIMIT = 32 * 1024 * 1024


def iota(shape, dim):
    return lax.broadcasted_iota(jnp.int32, shape, dim)


def split(values, terms):
    pieces = []
    for _ in range(terms - 1):
        pieces.append(values.astype(BF16))
        values = values - pieces[-1].astype(F32)
    return pieces + [values.astype(BF16)]


def joined(values, terms):
    total = values[:, 0:LANES]
    for i in range(1, terms):
        total = total + values[:, i * LANES : (i + 1) * LANES]
    return total


def one_hot(mask):
    return jnp.where(mask, 1.0, 0.0).astype(BF16)


def build_kernel(
    span_x,
    span_y,
    width,
    count,
    *refs,
):
    sources, refs = refs[:12], refs[12:]
    land_off, land_diag = refs[:2]
    inputs, refs = refs[2:14], refs[14:]
    (
        p_ref,
        m_ref,
        deriv_ref,
        acc_ref,
        trans_ref,
        up_ref,
        fsend_ref,
        fcell_ref,
        fslot_ref,
        ftrans_ref,
        fup_ref,
        owner_ref,
    ) = inputs
    (
        state_l,
        state_m,
        lower_y_l,
        lower_y_m,
        upper_y_l,
        upper_y_m,
        halo_out,
        halo_in,
        fault_out,
        fault_in,
        send_off,
        send_diag,
        input_sem,
        halo_ssem,
        halo_rsem,
        block_ssem,
        block_rsem,
        own_sem,
    ) = refs
    devices = span_x * span_y
    cells = width * width
    entries = count * count
    shift = width.bit_length() - 1
    lane_p, lane_t, lane_w = entries, entries + 1, entries + 3
    tx = lax.axis_index("tx")
    ty = lax.axis_index("ty")
    me = tx * span_y + ty

    loads = [
        pltpu.make_async_copy(source, target, input_sem.at[i])
        for i, (source, target) in enumerate(zip(sources, inputs))
    ]
    for load in loads:
        load.start()

    flips = []
    for code in range(span_y - 1, -1, -1):
        flipped = ty
        for bit in range(span_y.bit_length() - 1):
            if code >> bit & 1:
                flipped = flipped + (1 - 2 * (ty // (1 << bit) % 2)) * (1 << bit)
        flips.append(flipped)

    half = span_y // 2
    order = [flip for pair in zip(flips[:half], flips[half:]) for flip in pair]

    def each(function):
        def column_of(codes, step):
            x = tx + step
            x = x - jnp.where(x >= span_x, span_x, 0)
            for y in codes:
                function(x, y)

        def run(codes):
            def step_body(step, carry):
                column_of(codes, step)
                return carry

            lax.fori_loop(1, span_x, step_body, 0)

        column_of(order[: span_y - 1], 0)
        run(order)

    barrier = pltpu.get_barrier_semaphore()
    each(
        lambda x, y: pl.semaphore_signal(
            barrier, inc=1, device_id=(x, y), device_id_type=MESH
        )
    )

    def send_all(src, dst, kind):
        each(
            lambda x, y: pltpu.make_async_remote_copy(
                src_ref=src.at[x * span_y + y],
                dst_ref=dst.at[me],
                send_sem=block_ssem.at[kind],
                recv_sem=block_rsem.at[kind],
                device_id=(x, y),
                device_id_type=MESH,
            ).start()
        )

    def await_all(buffer, sem):
        span = buffer.at[pl.ds(0, devices - 1)]
        pltpu.make_async_copy(span, span, sem).wait()

    for load in loads:
        load.wait()

    fields = jnp.concatenate(
        [
            p_ref[...],
            m_ref[...],
            trans_ref[0 : 2 * width, :],
            up_ref[0 : 2 * width, :].astype(F32),
        ],
        0,
    )
    nfield = fields.shape[0]
    spread = one_hot((iota((cells, width), 0) & (width - 1)) == iota((cells, width), 1))
    crossed = lax.dot_general(
        jnp.concatenate([spread] * 3, 1),
        jnp.concatenate(split(fields, 3), 1),
        NT,
        preferred_element_type=F32,
    )
    same = (iota((cells, nfield), 1) & (width - 1)) == (iota((cells, nfield), 0) >> shift)
    kind = iota((nfield, LANES), 0) >> shift
    lane_of = jnp.where(
        kind == 0,
        lane_p,
        jnp.where(kind <= count, (kind - 1) * count, kind - (count + 1) + lane_t),
    )
    sorter = one_hot(iota((nfield, LANES), 1) == lane_of)
    misc = jnp.dot(
        jnp.concatenate(split(jnp.where(same, crossed, 0.0), 3), 1),
        jnp.concatenate([sorter] * 3, 0),
        preferred_element_type=F32,
    )
    state_m[...] = misc
    state_l[...] = jnp.zeros_like(state_l)
    state_l[:, 0:entries] = deriv_ref[...]
    deriv = state_l[...]

    last = cells - width
    halo_out[0, 0:width] = deriv[0:width]
    halo_out[0, width : 2 * width] = misc[0:width]
    halo_out[1, 0:width] = deriv[last:]
    halo_out[1, width : 2 * width] = misc[last:]
    for side, start in ((2, 0), (3, width - 1)):
        halo_out[side, 0:width] = state_l[pl.ds(start, width, stride=width), :]
        halo_out[side, width : 2 * width] = state_m[pl.ds(start, width, stride=width), :]

    ends = (tx > 0, tx < span_x - 1, ty > 0, ty < span_y - 1)
    targets = ((tx - 1, ty), (tx + 1, ty), (tx, ty - 1), (tx, ty + 1))

    def halo_copy(side):
        return pltpu.make_async_remote_copy(
            src_ref=halo_out.at[side],
            dst_ref=halo_in.at[side ^ 1],
            send_sem=halo_ssem.at[side],
            recv_sem=halo_rsem.at[side ^ 1],
            device_id=targets[side],
            device_id_type=MESH,
        )

    caps = fsend_ref.shape[0]
    slab = fault_out.shape[1]
    lines = devices * slab
    slab_shift = slab.bit_length() - 1
    widen = one_hot((iota((lines, devices), 0) >> slab_shift) == iota((lines, devices), 1))
    picks = lax.dot_general(
        widen, fsend_ref[...].astype(F32).astype(BF16), NT, preferred_element_type=F32
    )
    part = iota((lines, 1), 0) & (slab - 1)
    index = jnp.where((part & 1) == 0, picks[:, 0:1], picks[:, 1:2])
    hit = iota((lines, cells), 1).astype(F32) == index
    take_l = one_hot(hit & (part < caps))
    take_m = one_hot(hit & (part >= caps))
    gathered = joined(
        jnp.dot(take_l, jnp.concatenate(split(deriv, 2), 1), preferred_element_type=F32), 2
    ) + joined(
        jnp.dot(take_m, jnp.concatenate(split(misc, 3), 1), preferred_element_type=F32), 3
    )
    fault_out[...] = gathered.reshape(devices, slab, LANES)
    fault_in[pl.ds(me, 1)] = fault_out[pl.ds(me, 1)]


    owner = owner_ref[...]
    named = (iota((devices, cells), 0) == owner).astype(F32)
    before = one_hot(iota((cells, cells), 0) < iota((cells, cells), 1))
    earlier = jnp.dot(named.astype(BF16), before, preferred_element_type=F32)
    rank = jnp.sum(earlier * named, 0, keepdims=True)
    slot = owner.astype(F32) * ROWS + rank
    slots = devices * ROWS
    mover = one_hot(iota((slots, cells), 0).astype(F32) == slot)

    faults = fcell_ref.shape[1]
    chosen = (iota((cells, faults), 0) == fcell_ref[...]).astype(F32)
    fslot = fslot_ref[...]
    line = lax.div(fslot, caps) * slab + lax.rem(fslot, caps)

    def of_cell(values):
        return jnp.sum(chosen * values, 1, keepdims=True)

    base = of_cell(line.astype(F32))
    fault_conduct = of_cell(ftrans_ref[...])
    fault_flag = of_cell(fup_ref[...].astype(F32))
    where = iota((cells, lines), 1).astype(F32)
    pull_l = one_hot(where == base)
    pull_m = one_hot(where == base + caps)

    pl.semaphore_wait(barrier, devices - 1)
    for side in range(4):
        pl.when(ends[side])(lambda side=side: halo_copy(side).start())
    send_all(fault_out, fault_in, 0)

    pressure = misc[:, lane_p : lane_p + 1]
    row = iota((cells, 1), 0)
    at_x = row >> shift
    at_y = row & (width - 1)

    def terms(other_l, other_m, conduct, flag):
        lower = 1.0 - flag
        diff = pressure - other_m[:, lane_p : lane_p + 1]
        mu = (conduct * flag) * misc + (conduct * lower) * other_m
        off = (conduct * lower * diff) * other_l - mu
        return conduct * flag * diff, mu, off

    for side in range(4):
        @pl.when(ends[side])
        def _(side=side):
            halo_copy(side ^ 1).wait_recv()

        @pl.when(jnp.logical_not(ends[side]))
        def _(side=side):
            halo_in[side] = jnp.zeros_like(halo_in[side])

    def column(array, lane):
        return array[:, lane : lane + 1]

    near_l = jnp.concatenate([halo_in[0, 0:width], deriv[:last]], 0)
    near_m = jnp.concatenate([halo_in[0, width : 2 * width], misc[:last]], 0)
    far_l = jnp.concatenate([deriv[width:], halo_in[1, 0:width]], 0)
    far_m = jnp.concatenate([misc[width:], halo_in[1, width : 2 * width]], 0)
    for kept, field, rows, amount, start, side in (
        (lower_y_l, deriv, slice(0, width), 1, 0, 2),
        (lower_y_m, misc, slice(width, 2 * width), 1, 0, 2),
        (upper_y_l, deriv, slice(0, width), cells - 1, width - 1, 3),
        (upper_y_m, misc, slice(width, 2 * width), cells - 1, width - 1, 3),
    ):
        kept[...] = pltpu.roll(field, amount, 0)
        kept[pl.ds(start, width, stride=width), :] = halo_in[side, rows, :]

    keep_x = jnp.where((at_x < width - 1) | (tx < span_x - 1), 1.0, 0.0)
    keep_y = jnp.where((at_y < width - 1) | (ty < span_y - 1), 1.0, 0.0)
    low_y_m = lower_y_m[...]
    sides = (
        (near_l, near_m, column(near_m, lane_t), 1.0 - column(near_m, lane_w)),
        (far_l, far_m, column(misc, lane_t) * keep_x, column(misc, lane_w)),
        (
            lower_y_l[...],
            low_y_m,
            column(low_y_m, lane_t + 1),
            1.0 - column(low_y_m, lane_w + 1),
        ),
        (
            upper_y_l[...],
            upper_y_m[...],
            column(misc, lane_t + 1) * keep_y,
            column(misc, lane_w + 1),
        ),
    )
    scale = jnp.zeros((cells, 1), F32)
    mobile = jnp.zeros((cells, LANES), F32)
    offs = []
    for other_l, other_m, conduct, flag in sides:
        part_scale, mu, off = terms(other_l, other_m, conduct, flag)
        scale = scale + part_scale
        mobile = mobile + mu
        offs.append(off.astype(BF16))

    def place_rows(parts, buffer):
        moved = jnp.dot(
            mover, jnp.concatenate(parts, 1), preferred_element_type=F32
        ).astype(BF16)
        for i in range(len(parts)):
            buffer[:, i * ROWS : (i + 1) * ROWS, :] = moved[
                :, i * LANES : (i + 1) * LANES
            ].reshape(devices, ROWS, LANES)

    place_rows(offs, send_off)
    send_all(send_off, land_off, 1)
    own_off = pltpu.make_async_copy(send_off.at[me], land_off.at[me], own_sem.at[0])
    own_off.start()

    await_all(fault_in, block_rsem.at[0])
    arrived = fault_in[...].reshape(lines, LANES)
    pieces = split(arrived, 3)
    other_l = joined(
        jnp.dot(pull_l, jnp.concatenate(pieces[:2], 1), preferred_element_type=F32), 2
    )
    other_m = joined(
        jnp.dot(pull_m, jnp.concatenate(pieces, 1), preferred_element_type=F32), 3
    )
    part_scale, mu, off = terms(other_l, other_m, fault_conduct, fault_flag)
    diag = (scale + part_scale) * deriv + (mobile + mu)
    state_m[...] = diag
    state_m[:, 0:entries] = state_m[:, 0:entries] + acc_ref[...]
    place_rows([state_m[...].astype(BF16), off.astype(BF16)], send_diag)
    send_all(send_diag, land_diag, 2)
    own_diag = pltpu.make_async_copy(send_diag.at[me], land_diag.at[me], own_sem.at[1])
    own_diag.start()

    for side in range(4):
        pl.when(ends[side])(lambda side=side: halo_copy(side).wait_send())
    await_all(fault_out, block_ssem.at[0])
    await_all(send_off, block_ssem.at[1])
    await_all(send_diag, block_ssem.at[2])
    own_off.wait()
    own_diag.wait()
    await_all(land_off, block_rsem.at[1])
    await_all(land_diag, block_rsem.at[2])


def expand_kernel(capacity, count, group, off_ref, diag_ref, out_hbm, order_ref, widen_ref, out_ref, sem):
    kinds = (off_ref.shape[1] + diag_ref.shape[1]) // ROWS
    tall = capacity * BLOCKS
    kind = iota((tall, kinds * ROWS), 1) // ROWS
    block = jnp.where(kind < 4, kind + 1, jnp.where(kind == 4, 0, BLOCKS - 1))
    rank = iota((tall, kinds * ROWS), 1) % ROWS
    line = iota((tall, kinds * ROWS), 0)
    order_ref[...] = one_hot((line // BLOCKS == rank) & (line % BLOCKS == block))
    entry = iota((LANES, PAD * PAD), 0)
    target = entry // count * PAD + entry % count
    widen_ref[...] = one_hot((iota((LANES, PAD * PAD), 1) == target) & (entry < count * count))

    def piece(step, carry):
        first = step * group
        ordered = []
        for i in range(0, group, 2):
            pair = jnp.concatenate(
                [
                    jnp.concatenate([land[first + i], land[first + i + 1]], 1)
                    for land in (off_ref, diag_ref)
                ],
                0,
            )
            both = jnp.dot(order_ref[...], pair, preferred_element_type=F32).astype(BF16)
            ordered += [both[:, :LANES], both[:, LANES:]]
        full = jnp.dot(jnp.concatenate(ordered, 0), widen_ref[...], preferred_element_type=F32)
        out_ref[pl.ds(first * capacity, group * capacity)] = full.astype(BF16).reshape(
            group * capacity, BLOCKS, PAD * PAD
        )
        for i in range(group):
            rows = pl.ds((first + i) * capacity, capacity)
            pltpu.make_async_copy(out_ref.at[rows], out_hbm.at[rows], sem.at[0]).start()
        return carry

    lax.fori_loop(0, off_ref.shape[0] // group, piece, 0)
    pltpu.make_async_copy(out_ref, out_hbm, sem.at[0]).wait()


def body(
    span_x,
    span_y,
    pressure,
    mobility,
    mob_deriv,
    accum,
    trans,
    upwind,
    fault_send,
    fault_cell,
    fault_slot,
    fault_trans,
    fault_up,
    cell_owner,
):
    width = pressure.shape[0]
    count = mobility.shape[0]
    cells = width * width
    devices = span_x * span_y
    capacity = max(2, 2 * cells // devices)
    caps = fault_send.shape[2]
    assert pressure.shape == (width, width, 1) and caps == 2
    entries = count * count
    vmem = pl.BlockSpec(memory_space=pltpu.VMEM)
    wide = pltpu.VMEM((cells, LANES), F32)
    sems = pltpu.SemaphoreType.DMA
    arrays = (
        pressure.reshape(width, width),
        mobility.reshape(count * width, width),
        jnp.transpose(mob_deriv, (1, 2, 3, 0)).reshape(cells, entries),
        jnp.transpose(accum, (1, 2, 3, 0)).reshape(cells, entries),
        trans.reshape(3 * width, width),
        upwind.reshape(3 * width, width),
        jnp.transpose(fault_send, (0, 2, 1)).reshape(caps, devices),
        fault_cell,
        fault_slot,
        fault_trans,
        fault_up,
        cell_owner.reshape(1, cells),
    )
    land_off, land_diag = pl.pallas_call(
        functools.partial(build_kernel, span_x, span_y, width, count),
        out_shape=(
            pltpu.VMEM((devices, 4 * ROWS, LANES), BF16),
            pltpu.VMEM((devices, 2 * ROWS, LANES), BF16),
        ),
        in_specs=[pl.BlockSpec(memory_space=pltpu.HBM)] * 12,
        out_specs=(vmem, vmem),
        scratch_shapes=[pltpu.VMEM(array.shape, array.dtype) for array in arrays]
        + [wide] * 6
        + [
            pltpu.VMEM((4, 2 * width, LANES), F32),
            pltpu.VMEM((4, 2 * width, LANES), F32),
            pltpu.VMEM((devices, 2 * caps, LANES), F32),
            pltpu.VMEM((devices, 2 * caps, LANES), F32),
            pltpu.VMEM((devices, 4 * ROWS, LANES), BF16),
            pltpu.VMEM((devices, 2 * ROWS, LANES), BF16),
            sems((len(arrays),)),
            sems((4,)),
            sems((4,)),
            sems((3,)),
            sems((3,)),
            sems((2,)),
        ],
        compiler_params=pltpu.CompilerParams(
            collective_id=0, has_side_effects=True, vmem_limit_bytes=VMEM_LIMIT
        ),
        name="build_rows",
    )(*[pltpu.with_memory_space_constraint(array, pltpu.HBM) for array in arrays])
    group = devices // 8
    full = (devices * capacity, BLOCKS, PAD * PAD)
    return pl.pallas_call(
        functools.partial(expand_kernel, capacity, count, group),
        out_shape=jax.ShapeDtypeStruct(full, BF16),
        in_specs=[vmem] * 2,
        out_specs=pl.BlockSpec(memory_space=pltpu.HBM),
        scratch_shapes=[
            pltpu.VMEM((capacity * BLOCKS, 6 * ROWS), BF16),
            pltpu.VMEM((LANES, PAD * PAD), BF16),
            pltpu.VMEM(full, BF16),
            sems((1,)),
        ],
        compiler_params=pltpu.CompilerParams(vmem_limit_bytes=EXPAND_LIMIT),
        name="expand_rows",
    )(land_off, land_diag)


def solution(mesh):
    in_specs = (
        P("tx", "ty", None),
        P(None, "tx", "ty", None),
        P(None, "tx", "ty", None),
        P(None, "tx", "ty", None),
        P(None, "tx", "ty", None),
        P(None, "tx", "ty", None),
        P(("tx", "ty"), None, None),
        P(("tx", "ty"), None),
        P(("tx", "ty"), None),
        P(("tx", "ty"), None),
        P(("tx", "ty"), None),
        P(("tx", "ty"), None),
    )
    out_specs = P(("tx", "ty"), None, None)
    local = functools.partial(body, mesh.shape["tx"], mesh.shape["ty"])
    return jax.shard_map(local, mesh=mesh, in_specs=in_specs, out_specs=out_specs, check_vma=False)
```

```python
import functools

import jax
import jax.numpy as jnp
from jax import lax
from jax.experimental import pallas as pl
from jax.experimental.pallas import tpu as pltpu
from jax.sharding import PartitionSpec as P

PAD = 16
BLOCKS = 8
LANES = 128
ROWS = 16
MESH = pl.DeviceIdType.MESH
F32 = jnp.float32
BF16 = jnp.bfloat16
NT = (((1,), (1,)), ((), ()))
VMEM_LIMIT = 48 * 1024 * 1024
EXPAND_LIMIT = 32 * 1024 * 1024


def iota(shape, dim):
    return lax.broadcasted_iota(jnp.int32, shape, dim)


def split(values, terms):
    pieces = []
    for _ in range(terms - 1):
        pieces.append(values.astype(BF16))
        values = values - pieces[-1].astype(F32)
    return pieces + [values.astype(BF16)]


def joined(values, terms):
    total = values[:, 0:LANES]
    for i in range(1, terms):
        total = total + values[:, i * LANES : (i + 1) * LANES]
    return total


def one_hot(mask):
    return jnp.where(mask, 1.0, 0.0).astype(BF16)


def build_kernel(
    span_x,
    span_y,
    width,
    count,
    *refs,
):
    sources, refs = refs[:12], refs[12:]
    land, inputs, refs = refs[0], refs[1:13], refs[13:]
    (
        p_ref,
        m_ref,
        deriv_ref,
        acc_ref,
        trans_ref,
        up_ref,
        fsend_ref,
        fcell_ref,
        fslot_ref,
        ftrans_ref,
        fup_ref,
        owner_ref,
    ) = inputs
    (
        state_l,
        state_m,
        lower_y_l,
        lower_y_m,
        upper_y_l,
        upper_y_m,
        halo_out,
        halo_in,
        fault_out,
        fault_in,
        send,
        input_sem,
        halo_ssem,
        halo_rsem,
        block_ssem,
        block_rsem,
        own_sem,
    ) = refs
    devices = span_x * span_y
    cells = width * width
    entries = count * count
    shift = width.bit_length() - 1
    lane_p, lane_t, lane_w = entries, entries + 1, entries + 3
    tx = lax.axis_index("tx")
    ty = lax.axis_index("ty")
    me = tx * span_y + ty

    loads = [
        pltpu.make_async_copy(source, target, input_sem.at[i])
        for i, (source, target) in enumerate(zip(sources, inputs))
    ]
    for load in loads:
        load.start()

    flips = []
    for code in range(span_y - 1, -1, -1):
        flipped = ty
        for bit in range(span_y.bit_length() - 1):
            if code >> bit & 1:
                flipped = flipped + (1 - 2 * (ty // (1 << bit) % 2)) * (1 << bit)
        flips.append(flipped)

    half = span_y // 2
    across, near = flips[:half], flips[half:]

    def column_of(function, codes, step):
        x = tx + step
        x = x - jnp.where(x >= span_x, span_x, 0)
        for y in codes:
            function(x, y)

    def columns_of(function, codes, first):
        def step_body(step, carry):
            column_of(function, codes, step)
            return carry

        lax.fori_loop(first, span_x, step_body, 0)

    def each_across(function):
        columns_of(function, across, 0)

    def each_near(function):
        column_of(function, near[:-1], 0)
        columns_of(function, near, 1)

    def each(function):
        each_across(function)
        each_near(function)

    barrier = pltpu.get_barrier_semaphore()
    each(
        lambda x, y: pl.semaphore_signal(
            barrier, inc=1, device_id=(x, y), device_id_type=MESH
        )
    )

    def row_sender(start, size):
        lines = pl.ds(start, size)
        return lambda x, y: pltpu.make_async_remote_copy(
            src_ref=send.at[x * span_y + y, lines],
            dst_ref=land.at[me, lines],
            send_sem=block_ssem.at[1],
            recv_sem=block_rsem.at[1],
            device_id=(x, y),
            device_id_type=MESH,
        ).start()

    def fault_sender(x, y):
        pltpu.make_async_remote_copy(
            src_ref=fault_out.at[x * span_y + y],
            dst_ref=fault_in.at[me],
            send_sem=block_ssem.at[0],
            recv_sem=block_rsem.at[0],
            device_id=(x, y),
            device_id_type=MESH,
        ).start()

    def await_all(buffer, sem):
        span = buffer.at[pl.ds(0, devices - 1)]
        pltpu.make_async_copy(span, span, sem).wait()

    for load in loads:
        load.wait()

    fields = jnp.concatenate(
        [
            p_ref[...],
            m_ref[...],
            trans_ref[0 : 2 * width, :],
            up_ref[0 : 2 * width, :].astype(F32),
        ],
        0,
    )
    nfield = fields.shape[0]
    spread = one_hot((iota((cells, width), 0) & (width - 1)) == iota((cells, width), 1))
    crossed = lax.dot_general(
        jnp.concatenate([spread] * 3, 1),
        jnp.concatenate(split(fields, 3), 1),
        NT,
        preferred_element_type=F32,
    )
    same = (iota((cells, nfield), 1) & (width - 1)) == (iota((cells, nfield), 0) >> shift)
    kind = iota((nfield, LANES), 0) >> shift
    lane_of = jnp.where(
        kind == 0,
        lane_p,
        jnp.where(kind <= count, (kind - 1) * count, kind - (count + 1) + lane_t),
    )
    sorter = one_hot(iota((nfield, LANES), 1) == lane_of)
    misc = jnp.dot(
        jnp.concatenate(split(jnp.where(same, crossed, 0.0), 3), 1),
        jnp.concatenate([sorter] * 3, 0),
        preferred_element_type=F32,
    )
    state_m[...] = misc
    state_l[...] = jnp.zeros_like(state_l)
    state_l[:, 0:entries] = deriv_ref[...]
    deriv = state_l[...]

    last = cells - width
    halo_out[0, 0:width] = deriv[0:width]
    halo_out[0, width : 2 * width] = misc[0:width]
    halo_out[1, 0:width] = deriv[last:]
    halo_out[1, width : 2 * width] = misc[last:]
    for side, start in ((2, 0), (3, width - 1)):
        halo_out[side, 0:width] = state_l[pl.ds(start, width, stride=width), :]
        halo_out[side, width : 2 * width] = state_m[pl.ds(start, width, stride=width), :]

    ends = (tx > 0, tx < span_x - 1, ty > 0, ty < span_y - 1)
    targets = ((tx - 1, ty), (tx + 1, ty), (tx, ty - 1), (tx, ty + 1))

    def halo_copy(side):
        return pltpu.make_async_remote_copy(
            src_ref=halo_out.at[side],
            dst_ref=halo_in.at[side ^ 1],
            send_sem=halo_ssem.at[side],
            recv_sem=halo_rsem.at[side ^ 1],
            device_id=targets[side],
            device_id_type=MESH,
        )

    caps = fsend_ref.shape[0]
    slab = fault_out.shape[1]
    lines = devices * slab
    slab_shift = slab.bit_length() - 1
    widen = one_hot((iota((lines, devices), 0) >> slab_shift) == iota((lines, devices), 1))
    picks = lax.dot_general(
        widen, fsend_ref[...].astype(F32).astype(BF16), NT, preferred_element_type=F32
    )
    part = iota((lines, 1), 0) & (slab - 1)
    index = jnp.where((part & 1) == 0, picks[:, 0:1], picks[:, 1:2])
    hit = iota((lines, cells), 1).astype(F32) == index
    take_l = one_hot(hit & (part < caps))
    take_m = one_hot(hit & (part >= caps))
    gathered = joined(
        jnp.dot(take_l, jnp.concatenate(split(deriv, 2), 1), preferred_element_type=F32), 2
    ) + joined(
        jnp.dot(take_m, jnp.concatenate(split(misc, 3), 1), preferred_element_type=F32), 3
    )
    fault_out[...] = gathered.reshape(devices, slab, LANES)
    fault_in[pl.ds(me, 1)] = fault_out[pl.ds(me, 1)]


    owner = owner_ref[...]
    named = (iota((devices, cells), 0) == owner).astype(F32)
    before = one_hot(iota((cells, cells), 0) < iota((cells, cells), 1))
    earlier = jnp.dot(named.astype(BF16), before, preferred_element_type=F32)
    rank = jnp.sum(earlier * named, 0, keepdims=True)
    slot = owner.astype(F32) * ROWS + rank
    slots = devices * ROWS
    mover = one_hot(iota((slots, cells), 0).astype(F32) == slot)

    faults = fcell_ref.shape[1]
    chosen = (iota((cells, faults), 0) == fcell_ref[...]).astype(F32)
    fslot = fslot_ref[...]
    line = lax.div(fslot, caps) * slab + lax.rem(fslot, caps)

    def of_cell(values):
        return jnp.sum(chosen * values, 1, keepdims=True)

    base = of_cell(line.astype(F32))
    fault_conduct = of_cell(ftrans_ref[...])
    fault_flag = of_cell(fup_ref[...].astype(F32))
    where = iota((cells, lines), 1).astype(F32)
    pull_l = one_hot(where == base)
    pull_m = one_hot(where == base + caps)

    pl.semaphore_wait(barrier, devices - 1)
    for side in range(4):
        pl.when(ends[side])(lambda side=side: halo_copy(side).start())
    each(fault_sender)

    pressure = misc[:, lane_p : lane_p + 1]
    row = iota((cells, 1), 0)
    at_x = row >> shift
    at_y = row & (width - 1)

    def terms(other_l, other_m, conduct, flag):
        lower = 1.0 - flag
        diff = pressure - other_m[:, lane_p : lane_p + 1]
        mu = (conduct * flag) * misc + (conduct * lower) * other_m
        off = (conduct * lower * diff) * other_l - mu
        return conduct * flag * diff, mu, off

    for side in range(4):
        @pl.when(ends[side])
        def _(side=side):
            halo_copy(side ^ 1).wait_recv()

        @pl.when(jnp.logical_not(ends[side]))
        def _(side=side):
            halo_in[side] = jnp.zeros_like(halo_in[side])

    def column(array, lane):
        return array[:, lane : lane + 1]

    near_l = jnp.concatenate([halo_in[0, 0:width], deriv[:last]], 0)
    near_m = jnp.concatenate([halo_in[0, width : 2 * width], misc[:last]], 0)
    far_l = jnp.concatenate([deriv[width:], halo_in[1, 0:width]], 0)
    far_m = jnp.concatenate([misc[width:], halo_in[1, width : 2 * width]], 0)
    for kept, field, rows, amount, start, side in (
        (lower_y_l, deriv, slice(0, width), 1, 0, 2),
        (lower_y_m, misc, slice(width, 2 * width), 1, 0, 2),
        (upper_y_l, deriv, slice(0, width), cells - 1, width - 1, 3),
        (upper_y_m, misc, slice(width, 2 * width), cells - 1, width - 1, 3),
    ):
        kept[...] = pltpu.roll(field, amount, 0)
        kept[pl.ds(start, width, stride=width), :] = halo_in[side, rows, :]

    keep_x = jnp.where((at_x < width - 1) | (tx < span_x - 1), 1.0, 0.0)
    keep_y = jnp.where((at_y < width - 1) | (ty < span_y - 1), 1.0, 0.0)
    low_y_m = lower_y_m[...]
    sides = (
        (near_l, near_m, column(near_m, lane_t), 1.0 - column(near_m, lane_w)),
        (far_l, far_m, column(misc, lane_t) * keep_x, column(misc, lane_w)),
        (
            lower_y_l[...],
            low_y_m,
            column(low_y_m, lane_t + 1),
            1.0 - column(low_y_m, lane_w + 1),
        ),
        (
            upper_y_l[...],
            upper_y_m[...],
            column(misc, lane_t + 1) * keep_y,
            column(misc, lane_w + 1),
        ),
    )
    scale = jnp.zeros((cells, 1), F32)
    mobile = jnp.zeros((cells, LANES), F32)
    offs = []
    for other_l, other_m, conduct, flag in sides:
        part_scale, mu, off = terms(other_l, other_m, conduct, flag)
        scale = scale + part_scale
        mobile = mobile + mu
        offs.append(off.astype(BF16))

    def place_rows(parts, first):
        moved = jnp.dot(
            mover, jnp.concatenate(parts, 1), preferred_element_type=F32
        ).astype(BF16)
        for i in range(len(parts)):
            start = (first + i) * ROWS
            send[:, start : start + ROWS, :] = moved[:, i * LANES : (i + 1) * LANES].reshape(
                devices, ROWS, LANES
            )

    early = 4 * ROWS
    late = 2 * ROWS
    place_rows(offs, 0)
    each_across(row_sender(0, early))

    await_all(fault_in, block_rsem.at[0])
    arrived = fault_in[...].reshape(lines, LANES)
    pieces = split(arrived, 3)
    other_l = joined(
        jnp.dot(pull_l, jnp.concatenate(pieces[:2], 1), preferred_element_type=F32), 2
    )
    other_m = joined(
        jnp.dot(pull_m, jnp.concatenate(pieces, 1), preferred_element_type=F32), 3
    )
    part_scale, mu, off = terms(other_l, other_m, fault_conduct, fault_flag)
    diag = (scale + part_scale) * deriv + (mobile + mu)
    state_m[...] = diag
    state_m[:, 0:entries] = state_m[:, 0:entries] + acc_ref[...]
    place_rows([state_m[...].astype(BF16), off.astype(BF16)], 4)
    each_across(row_sender(early, late))
    each_near(row_sender(0, early + late))
    own = pltpu.make_async_copy(send.at[me], land.at[me], own_sem.at[0])
    own.start()

    for side in range(4):
        pl.when(ends[side])(lambda side=side: halo_copy(side).wait_send())
    await_all(fault_out, block_ssem.at[0])
    await_all(send, block_ssem.at[1])
    own.wait()
    await_all(land, block_rsem.at[1])


def expand_kernel(capacity, count, group, land, out_ref):
    kinds = land.shape[1] // ROWS
    tall = capacity * BLOCKS
    kind = iota((tall, kinds * ROWS), 1) // ROWS
    block = jnp.where(kind < 4, kind + 1, jnp.where(kind == 4, 0, BLOCKS - 1))
    rank = iota((tall, kinds * ROWS), 1) % ROWS
    line = iota((tall, kinds * ROWS), 0)
    order = one_hot((line // BLOCKS == rank) & (line % BLOCKS == block))
    entry = iota((LANES, PAD * PAD), 0)
    target = entry // count * PAD + entry % count
    widen = one_hot((iota((LANES, PAD * PAD), 1) == target) & (entry < count * count))
    first = pl.program_id(0) * group
    ordered = []
    for i in range(0, group, 2):
        pair = jnp.concatenate([land[first + i], land[first + i + 1]], 1)
        both = jnp.dot(order, pair, preferred_element_type=F32).astype(BF16)
        ordered += [both[:, :LANES], both[:, LANES:]]
    full = jnp.dot(jnp.concatenate(ordered, 0), widen, preferred_element_type=F32)
    out_ref[...] = full.astype(BF16).reshape(group * capacity, BLOCKS, PAD * PAD)


def body(
    span_x,
    span_y,
    pressure,
    mobility,
    mob_deriv,
    accum,
    trans,
    upwind,
    fault_send,
    fault_cell,
    fault_slot,
    fault_trans,
    fault_up,
    cell_owner,
):
    width = pressure.shape[0]
    count = mobility.shape[0]
    cells = width * width
    devices = span_x * span_y
    capacity = max(2, 2 * cells // devices)
    caps = fault_send.shape[2]
    assert pressure.shape == (width, width, 1) and caps == 2
    entries = count * count
    vmem = pl.BlockSpec(memory_space=pltpu.VMEM)
    wide = pltpu.VMEM((cells, LANES), F32)
    sems = pltpu.SemaphoreType.DMA
    arrays = (
        pressure.reshape(width, width),
        mobility.reshape(count * width, width),
        jnp.transpose(mob_deriv, (1, 2, 3, 0)).reshape(cells, entries),
        jnp.transpose(accum, (1, 2, 3, 0)).reshape(cells, entries),
        trans.reshape(3 * width, width),
        upwind.reshape(3 * width, width),
        jnp.transpose(fault_send, (0, 2, 1)).reshape(caps, devices),
        fault_cell,
        fault_slot,
        fault_trans,
        fault_up,
        cell_owner.reshape(1, cells),
    )
    land = pl.pallas_call(
        functools.partial(build_kernel, span_x, span_y, width, count),
        out_shape=pltpu.VMEM((devices, 6 * ROWS, LANES), BF16),
        in_specs=[pl.BlockSpec(memory_space=pltpu.HBM)] * 12,
        out_specs=vmem,
        scratch_shapes=[pltpu.VMEM(array.shape, array.dtype) for array in arrays]
        + [wide] * 6
        + [
            pltpu.VMEM((4, 2 * width, LANES), F32),
            pltpu.VMEM((4, 2 * width, LANES), F32),
            pltpu.VMEM((devices, 2 * caps, LANES), F32),
            pltpu.VMEM((devices, 2 * caps, LANES), F32),
            pltpu.VMEM((devices, 6 * ROWS, LANES), BF16),
            sems((len(arrays),)),
            sems((4,)),
            sems((4,)),
            sems((2,)),
            sems((2,)),
            sems((1,)),
        ],
        compiler_params=pltpu.CompilerParams(
            collective_id=0, has_side_effects=True, vmem_limit_bytes=VMEM_LIMIT
        ),
        name="build_rows",
    )(*[pltpu.with_memory_space_constraint(array, pltpu.HBM) for array in arrays])
    group = devices // 4
    full = (devices * capacity, BLOCKS, PAD * PAD)
    return pl.pallas_call(
        functools.partial(expand_kernel, capacity, count, group),
        grid=(devices // group,),
        out_shape=jax.ShapeDtypeStruct(full, BF16),
        in_specs=[vmem],
        out_specs=pl.BlockSpec((group * capacity,) + full[1:], lambda i: (i, 0, 0)),
        compiler_params=pltpu.CompilerParams(vmem_limit_bytes=EXPAND_LIMIT),
        name="expand_rows",
    )(land)


def solution(mesh):
    in_specs = (
        P("tx", "ty", None),
        P(None, "tx", "ty", None),
        P(None, "tx", "ty", None),
        P(None, "tx", "ty", None),
        P(None, "tx", "ty", None),
        P(None, "tx", "ty", None),
        P(("tx", "ty"), None, None),
        P(("tx", "ty"), None),
        P(("tx", "ty"), None),
        P(("tx", "ty"), None),
        P(("tx", "ty"), None),
        P(("tx", "ty"), None),
    )
    out_specs = P(("tx", "ty"), None, None)
    local = functools.partial(body, mesh.shape["tx"], mesh.shape["ty"])
    return jax.shard_map(local, mesh=mesh, in_specs=in_specs, out_specs=out_specs, check_vma=False)
```

```python
import functools

import jax
import jax.numpy as jnp
from jax import lax
from jax.experimental import pallas as pl
from jax.experimental.pallas import tpu as pltpu
from jax.sharding import PartitionSpec as P

PAD = 16
BLOCKS = 8
LANES = 128
ROWS = 16
MESH = pl.DeviceIdType.MESH
F32 = jnp.float32
BF16 = jnp.bfloat16
NT = (((1,), (1,)), ((), ()))
VMEM_LIMIT = 48 * 1024 * 1024
EXPAND_LIMIT = 32 * 1024 * 1024


def iota(shape, dim):
    return lax.broadcasted_iota(jnp.int32, shape, dim)


def split(values, terms):
    pieces = []
    for _ in range(terms - 1):
        pieces.append(values.astype(BF16))
        values = values - pieces[-1].astype(F32)
    return pieces + [values.astype(BF16)]


def joined(values, terms):
    total = values[:, 0:LANES]
    for i in range(1, terms):
        total = total + values[:, i * LANES : (i + 1) * LANES]
    return total


def one_hot(mask):
    return jnp.where(mask, 1.0, 0.0).astype(BF16)


def build_kernel(
    span_x,
    span_y,
    width,
    count,
    *refs,
):
    sources, refs = refs[:12], refs[12:]
    land, inputs, refs = refs[0], refs[1:13], refs[13:]
    (
        p_ref,
        m_ref,
        deriv_ref,
        acc_ref,
        trans_ref,
        up_ref,
        fsend_ref,
        fcell_ref,
        fslot_ref,
        ftrans_ref,
        fup_ref,
        owner_ref,
    ) = inputs
    (
        state_l,
        state_m,
        near_l,
        near_m,
        rates,
        offs,
        total,
        halo_out,
        halo_in,
        fault_out,
        fault_in,
        send,
        input_sem,
        halo_ssem,
        halo_rsem,
        block_ssem,
        block_rsem,
        own_sem,
    ) = refs
    devices = span_x * span_y
    cells = width * width
    entries = count * count
    shift = width.bit_length() - 1
    lane_p, lane_t, lane_w = entries, entries + 1, entries + 3
    tx = lax.axis_index("tx")
    ty = lax.axis_index("ty")
    me = tx * span_y + ty

    loads = [
        pltpu.make_async_copy(source, target, input_sem.at[i])
        for i, (source, target) in enumerate(zip(sources, inputs))
    ]
    for load in loads:
        load.start()

    flips = []
    for code in range(span_y - 1, -1, -1):
        flipped = ty
        for bit in range(span_y.bit_length() - 1):
            if code >> bit & 1:
                flipped = flipped + (1 - 2 * (ty // (1 << bit) % 2)) * (1 << bit)
        flips.append(flipped)

    half = span_y // 2
    across, near = flips[:half], flips[half:]

    def column_of(function, codes, step):
        x = tx + step
        x = x - jnp.where(x >= span_x, span_x, 0)
        for y in codes:
            function(x, y)

    def columns_of(function, codes, first):
        def step_body(step, carry):
            column_of(function, codes, step)
            return carry

        lax.fori_loop(first, span_x, step_body, 0)

    def each_across(function):
        columns_of(function, across, 0)

    def each_near(function):
        column_of(function, near[:-1], 0)
        columns_of(function, near, 1)

    def each(function):
        each_across(function)
        each_near(function)

    barrier = pltpu.get_barrier_semaphore()
    each(
        lambda x, y: pl.semaphore_signal(
            barrier, inc=1, device_id=(x, y), device_id_type=MESH
        )
    )

    def row_sender(start, size):
        lines = pl.ds(start, size)
        return lambda x, y: pltpu.make_async_remote_copy(
            src_ref=send.at[x * span_y + y, lines],
            dst_ref=land.at[me, lines],
            send_sem=block_ssem.at[1],
            recv_sem=block_rsem.at[1],
            device_id=(x, y),
            device_id_type=MESH,
        ).start()

    def fault_sender(x, y):
        pltpu.make_async_remote_copy(
            src_ref=fault_out.at[x * span_y + y],
            dst_ref=fault_in.at[me],
            send_sem=block_ssem.at[0],
            recv_sem=block_rsem.at[0],
            device_id=(x, y),
            device_id_type=MESH,
        ).start()

    def await_all(buffer, sem):
        span = buffer.at[pl.ds(0, devices - 1)]
        pltpu.make_async_copy(span, span, sem).wait()

    for load in loads:
        load.wait()

    fields = jnp.concatenate(
        [
            p_ref[...],
            m_ref[...],
            trans_ref[0 : 2 * width, :],
            up_ref[0 : 2 * width, :].astype(F32),
        ],
        0,
    )
    nfield = fields.shape[0]
    spread = one_hot((iota((cells, width), 0) & (width - 1)) == iota((cells, width), 1))
    crossed = lax.dot_general(
        jnp.concatenate([spread] * 3, 1),
        jnp.concatenate(split(fields, 3), 1),
        NT,
        preferred_element_type=F32,
    )
    same = (iota((cells, nfield), 1) & (width - 1)) == (iota((cells, nfield), 0) >> shift)
    kind = iota((nfield, LANES), 0) >> shift
    lane_of = jnp.where(
        kind == 0,
        lane_p,
        jnp.where(kind <= count, (kind - 1) * count, kind - (count + 1) + lane_t),
    )
    sorter = one_hot(iota((nfield, LANES), 1) == lane_of)
    misc = jnp.dot(
        jnp.concatenate(split(jnp.where(same, crossed, 0.0), 3), 1),
        jnp.concatenate([sorter] * 3, 0),
        preferred_element_type=F32,
    )
    state_m[...] = misc
    state_l[...] = jnp.zeros_like(state_l)
    state_l[:, 0:entries] = deriv_ref[...]
    deriv = state_l[...]

    last = cells - width
    halo_out[0, 0:width] = deriv[0:width]
    halo_out[0, width : 2 * width] = misc[0:width]
    halo_out[1, 0:width] = deriv[last:]
    halo_out[1, width : 2 * width] = misc[last:]
    for side, start in ((2, 0), (3, width - 1)):
        halo_out[side, 0:width] = state_l[pl.ds(start, width, stride=width), :]
        halo_out[side, width : 2 * width] = state_m[pl.ds(start, width, stride=width), :]

    ends = (tx > 0, tx < span_x - 1, ty > 0, ty < span_y - 1)
    targets = ((tx - 1, ty), (tx + 1, ty), (tx, ty - 1), (tx, ty + 1))

    def halo_copy(side):
        return pltpu.make_async_remote_copy(
            src_ref=halo_out.at[side],
            dst_ref=halo_in.at[side ^ 1],
            send_sem=halo_ssem.at[side],
            recv_sem=halo_rsem.at[side ^ 1],
            device_id=targets[side],
            device_id_type=MESH,
        )

    caps = fsend_ref.shape[0]
    slab = fault_out.shape[1]
    lines = devices * slab
    slab_shift = slab.bit_length() - 1
    widen = one_hot((iota((lines, devices), 0) >> slab_shift) == iota((lines, devices), 1))
    picks = lax.dot_general(
        widen, fsend_ref[...].astype(F32).astype(BF16), NT, preferred_element_type=F32
    )
    part = iota((lines, 1), 0) & (slab - 1)
    index = jnp.where((part & 1) == 0, picks[:, 0:1], picks[:, 1:2])
    hit = iota((lines, cells), 1).astype(F32) == index
    take_l = one_hot(hit & (part < caps))
    take_m = one_hot(hit & (part >= caps))
    gathered = joined(
        jnp.dot(take_l, jnp.concatenate(split(deriv, 2), 1), preferred_element_type=F32), 2
    ) + joined(
        jnp.dot(take_m, jnp.concatenate(split(misc, 3), 1), preferred_element_type=F32), 3
    )
    fault_out[...] = gathered.reshape(devices, slab, LANES)
    fault_in[pl.ds(me, 1)] = fault_out[pl.ds(me, 1)]


    owner = owner_ref[...]
    named = (iota((devices, cells), 0) == owner).astype(F32)
    before = one_hot(iota((cells, cells), 0) < iota((cells, cells), 1))
    earlier = jnp.dot(named.astype(BF16), before, preferred_element_type=F32)
    rank = jnp.sum(earlier * named, 0, keepdims=True)
    slot = owner.astype(F32) * ROWS + rank
    slots = devices * ROWS
    mover = one_hot(iota((slots, cells), 0).astype(F32) == slot)

    faults = fcell_ref.shape[1]
    chosen = (iota((cells, faults), 0) == fcell_ref[...]).astype(F32)
    fslot = fslot_ref[...]
    line = lax.div(fslot, caps) * slab + lax.rem(fslot, caps)

    def of_cell(values):
        return jnp.sum(chosen * values, 1, keepdims=True)

    base = of_cell(line.astype(F32))
    fault_conduct = of_cell(ftrans_ref[...])
    fault_flag = of_cell(fup_ref[...].astype(F32))
    where = iota((cells, lines), 1).astype(F32)
    pull_l = one_hot(where == base)
    pull_m = one_hot(where == base + caps)

    row = iota((cells, 1), 0)
    at_x = row >> shift
    at_y = row & (width - 1)

    def column(array, lane):
        return array[:, lane : lane + 1]

    def terms(own_l, own_m, other_l, other_m, conduct, flag):
        lower = 1.0 - flag
        diff = column(own_m, lane_p) - column(other_m, lane_p)
        mu = (conduct * flag) * own_m + (conduct * lower) * other_m
        off = (conduct * lower * diff) * other_l - mu
        return (conduct * flag * diff) * own_l + mu, off

    for kept, field in ((near_l, deriv), (near_m, misc)):
        kept[0, width:] = field[:last]
        kept[0, 0:width] = jnp.zeros((width, LANES), F32)
        kept[1, 0:last] = field[width:]
        kept[1, last:] = jnp.zeros((width, LANES), F32)
        kept[2] = pltpu.roll(field, 1, 0)
        kept[3] = pltpu.roll(field, cells - 1, 0)
    inside = (at_x > 0, at_x < width - 1, at_y > 0, at_y < width - 1)
    for side in range(4):
        axis = side // 2
        if side % 2:
            conduct, flag = column(misc, lane_t + axis), column(misc, lane_w + axis)
        else:
            lower_m = near_m[side]
            conduct = column(lower_m, lane_t + axis)
            flag = 1.0 - column(lower_m, lane_w + axis)
        rates[side, :, 0:1] = jnp.where(inside[side], conduct, 0.0)
        rates[side, :, 1:2] = flag
    total[...] = jnp.zeros_like(total)
    total[:, 0:entries] = acc_ref[...]

    def inner(side, carry):
        rate = rates[side]
        added, off = terms(
            state_l[...],
            state_m[...],
            near_l[side],
            near_m[side],
            column(rate, 0),
            column(rate, 1),
        )
        total[...] += added
        offs[side] = off
        return carry

    lax.fori_loop(0, 4, inner, 0)

    pl.semaphore_wait(barrier, devices - 1)
    for side in range(4):
        pl.when(ends[side])(lambda side=side: halo_copy(side).start())
    each(fault_sender)

    for side in range(4):
        @pl.when(ends[side])
        def _(side=side):
            halo_copy(side ^ 1).wait_recv()

        @pl.when(jnp.logical_not(ends[side]))
        def _(side=side):
            halo_in[side] = jnp.zeros_like(halo_in[side])

    for side, rows in enumerate(
        (
            pl.ds(0, width),
            pl.ds(last, width),
            pl.ds(0, width, stride=width),
            pl.ds(width - 1, width, stride=width),
        )
    ):
        axis = side // 2
        own_l, own_m = state_l[rows, :], state_m[rows, :]
        other_l = halo_in[side, 0:width]
        other_m = halo_in[side, width : 2 * width]
        if side % 2:
            conduct = column(own_m, lane_t + axis) * jnp.where(ends[side], 1.0, 0.0)
            flag = column(own_m, lane_w + axis)
        else:
            conduct = column(other_m, lane_t + axis)
            flag = 1.0 - column(other_m, lane_w + axis)
        added, off = terms(own_l, own_m, other_l, other_m, conduct, flag)
        total[rows, :] = total[rows, :] + added
        offs[side, rows, :] = off

    def place_rows(parts, first):
        moved = jnp.dot(
            mover, jnp.concatenate(parts, 1), preferred_element_type=F32
        ).astype(BF16)
        for i in range(len(parts)):
            start = (first + i) * ROWS
            send[:, start : start + ROWS, :] = moved[:, i * LANES : (i + 1) * LANES].reshape(
                devices, ROWS, LANES
            )

    early = 4 * ROWS
    late = 2 * ROWS
    place_rows([offs[side].astype(BF16) for side in range(4)], 0)
    each_across(row_sender(0, early))

    await_all(fault_in, block_rsem.at[0])
    arrived = fault_in[...].reshape(lines, LANES)
    pieces = split(arrived, 3)
    other_l = joined(
        jnp.dot(pull_l, jnp.concatenate(pieces[:2], 1), preferred_element_type=F32), 2
    )
    other_m = joined(
        jnp.dot(pull_m, jnp.concatenate(pieces, 1), preferred_element_type=F32), 3
    )
    added, off = terms(
        state_l[...], state_m[...], other_l, other_m, fault_conduct, fault_flag
    )
    place_rows([(total[...] + added).astype(BF16), off.astype(BF16)], 4)
    each_across(row_sender(early, late))
    each_near(row_sender(0, early + late))
    own = pltpu.make_async_copy(send.at[me], land.at[me], own_sem.at[0])
    own.start()

    for side in range(4):
        pl.when(ends[side])(lambda side=side: halo_copy(side).wait_send())
    await_all(fault_out, block_ssem.at[0])
    await_all(send, block_ssem.at[1])
    own.wait()
    await_all(land, block_rsem.at[1])


def expand_kernel(capacity, count, group, land, out_ref):
    kinds = land.shape[1] // ROWS
    tall = capacity * BLOCKS
    kind = iota((tall, kinds * ROWS), 1) // ROWS
    block = jnp.where(kind < 4, kind + 1, jnp.where(kind == 4, 0, BLOCKS - 1))
    rank = iota((tall, kinds * ROWS), 1) % ROWS
    line = iota((tall, kinds * ROWS), 0)
    order = one_hot((line // BLOCKS == rank) & (line % BLOCKS == block))
    entry = iota((LANES, PAD * PAD), 0)
    target = entry // count * PAD + entry % count
    widen = one_hot((iota((LANES, PAD * PAD), 1) == target) & (entry < count * count))
    first = pl.program_id(0) * group
    ordered = []
    for i in range(0, group, 2):
        pair = jnp.concatenate([land[first + i], land[first + i + 1]], 1)
        both = jnp.dot(order, pair, preferred_element_type=F32).astype(BF16)
        ordered += [both[:, :LANES], both[:, LANES:]]
    full = jnp.dot(jnp.concatenate(ordered, 0), widen, preferred_element_type=F32)
    out_ref[...] = full.astype(BF16).reshape(group * capacity, BLOCKS, PAD * PAD)


def body(
    span_x,
    span_y,
    pressure,
    mobility,
    mob_deriv,
    accum,
    trans,
    upwind,
    fault_send,
    fault_cell,
    fault_slot,
    fault_trans,
    fault_up,
    cell_owner,
):
    width = pressure.shape[0]
    count = mobility.shape[0]
    cells = width * width
    devices = span_x * span_y
    capacity = max(2, 2 * cells // devices)
    caps = fault_send.shape[2]
    assert pressure.shape == (width, width, 1) and caps == 2
    entries = count * count
    vmem = pl.BlockSpec(memory_space=pltpu.VMEM)
    wide = pltpu.VMEM((cells, LANES), F32)
    sems = pltpu.SemaphoreType.DMA
    arrays = (
        pressure.reshape(width, width),
        mobility.reshape(count * width, width),
        jnp.transpose(mob_deriv, (1, 2, 3, 0)).reshape(cells, entries),
        jnp.transpose(accum, (1, 2, 3, 0)).reshape(cells, entries),
        trans.reshape(3 * width, width),
        upwind.reshape(3 * width, width),
        jnp.transpose(fault_send, (0, 2, 1)).reshape(caps, devices),
        fault_cell,
        fault_slot,
        fault_trans,
        fault_up,
        cell_owner.reshape(1, cells),
    )
    land = pl.pallas_call(
        functools.partial(build_kernel, span_x, span_y, width, count),
        out_shape=pltpu.VMEM((devices, 6 * ROWS, LANES), BF16),
        in_specs=[pl.BlockSpec(memory_space=pltpu.HBM)] * 12,
        out_specs=vmem,
        scratch_shapes=[pltpu.VMEM(array.shape, array.dtype) for array in arrays]
        + [wide] * 2
        + [pltpu.VMEM((4, cells, LANES), F32)] * 4
        + [wide]
        + [
            pltpu.VMEM((4, 2 * width, LANES), F32),
            pltpu.VMEM((4, 2 * width, LANES), F32),
            pltpu.VMEM((devices, 2 * caps, LANES), F32),
            pltpu.VMEM((devices, 2 * caps, LANES), F32),
            pltpu.VMEM((devices, 6 * ROWS, LANES), BF16),
            sems((len(arrays),)),
            sems((4,)),
            sems((4,)),
            sems((2,)),
            sems((2,)),
            sems((1,)),
        ],
        compiler_params=pltpu.CompilerParams(
            collective_id=0, has_side_effects=True, vmem_limit_bytes=VMEM_LIMIT
        ),
        name="build_rows",
    )(*[pltpu.with_memory_space_constraint(array, pltpu.HBM) for array in arrays])
    group = devices // 4
    full = (devices * capacity, BLOCKS, PAD * PAD)
    return pl.pallas_call(
        functools.partial(expand_kernel, capacity, count, group),
        grid=(devices // group,),
        out_shape=jax.ShapeDtypeStruct(full, BF16),
        in_specs=[vmem],
        out_specs=pl.BlockSpec((group * capacity,) + full[1:], lambda i: (i, 0, 0)),
        compiler_params=pltpu.CompilerParams(vmem_limit_bytes=EXPAND_LIMIT),
        name="expand_rows",
    )(land)


def solution(mesh):
    in_specs = (
        P("tx", "ty", None),
        P(None, "tx", "ty", None),
        P(None, "tx", "ty", None),
        P(None, "tx", "ty", None),
        P(None, "tx", "ty", None),
        P(None, "tx", "ty", None),
        P(("tx", "ty"), None, None),
        P(("tx", "ty"), None),
        P(("tx", "ty"), None),
        P(("tx", "ty"), None),
        P(("tx", "ty"), None),
        P(("tx", "ty"), None),
    )
    out_specs = P(("tx", "ty"), None, None)
    local = functools.partial(body, mesh.shape["tx"], mesh.shape["ty"])
    return jax.shard_map(local, mesh=mesh, in_specs=in_specs, out_specs=out_specs, check_vma=False)
```

```python
import functools

import jax
import jax.numpy as jnp
from jax import lax
from jax.experimental import pallas as pl
from jax.experimental.pallas import tpu as pltpu
from jax.sharding import PartitionSpec as P

PAD = 16
BLOCKS = 8
LANES = 128
ROWS = 16
MESH = pl.DeviceIdType.MESH
F32 = jnp.float32
BF16 = jnp.bfloat16
NT = (((1,), (1,)), ((), ()))
VMEM_LIMIT = 48 * 1024 * 1024
EXPAND_LIMIT = 32 * 1024 * 1024


def iota(shape, dim):
    return lax.broadcasted_iota(jnp.int32, shape, dim)


def split(values, terms):
    pieces = []
    for _ in range(terms - 1):
        pieces.append(values.astype(BF16))
        values = values - pieces[-1].astype(F32)
    return pieces + [values.astype(BF16)]


def joined(values, terms):
    total = values[:, 0:LANES]
    for i in range(1, terms):
        total = total + values[:, i * LANES : (i + 1) * LANES]
    return total


def one_hot(mask):
    return jnp.where(mask, 1.0, 0.0).astype(BF16)


def build_kernel(
    span_x,
    span_y,
    width,
    count,
    *refs,
):
    sources, refs = refs[:12], refs[12:]
    land, inputs, refs = refs[0], refs[1:13], refs[13:]
    (
        p_ref,
        m_ref,
        deriv_ref,
        acc_ref,
        trans_ref,
        up_ref,
        fsend_ref,
        fcell_ref,
        fslot_ref,
        ftrans_ref,
        fup_ref,
        owner_ref,
    ) = inputs
    (
        state_l,
        state_m,
        near_l,
        near_m,
        rates,
        offs,
        total,
        halo_out,
        halo_in,
        fault_out,
        fault_in,
        send,
        input_sem,
        halo_ssem,
        halo_rsem,
        block_ssem,
        block_rsem,
        own_sem,
    ) = refs
    devices = span_x * span_y
    cells = width * width
    entries = count * count
    shift = width.bit_length() - 1
    lane_p, lane_t, lane_w = entries, entries + 1, entries + 3
    tx = lax.axis_index("tx")
    ty = lax.axis_index("ty")
    me = tx * span_y + ty

    loads = [
        pltpu.make_async_copy(source, target, input_sem.at[i])
        for i, (source, target) in enumerate(zip(sources, inputs))
    ]
    for load in loads:
        load.start()

    flips = []
    for code in range(span_y - 1, -1, -1):
        flipped = ty
        for bit in range(span_y.bit_length() - 1):
            if code >> bit & 1:
                flipped = flipped + (1 - 2 * (ty // (1 << bit) % 2)) * (1 << bit)
        flips.append(flipped)

    half = span_y // 2
    across, near = flips[:half], flips[half:]

    def column_of(function, codes, step):
        x = tx + step
        x = x - jnp.where(x >= span_x, span_x, 0)
        for y in codes:
            function(x, y)

    def columns_of(function, codes, first):
        def step_body(step, carry):
            column_of(function, codes, step)
            return carry

        lax.fori_loop(first, span_x, step_body, 0)

    def each_across(function):
        columns_of(function, across, 0)

    def each_near(function):
        column_of(function, near[:-1], 0)
        columns_of(function, near, 1)

    def each(function):
        each_across(function)
        each_near(function)

    barrier = pltpu.get_barrier_semaphore()
    each(
        lambda x, y: pl.semaphore_signal(
            barrier, inc=1, device_id=(x, y), device_id_type=MESH
        )
    )

    def row_sender(start, size):
        lines = pl.ds(start, size)
        return lambda x, y: pltpu.make_async_remote_copy(
            src_ref=send.at[x * span_y + y, lines],
            dst_ref=land.at[me, lines],
            send_sem=block_ssem.at[1],
            recv_sem=block_rsem.at[1],
            device_id=(x, y),
            device_id_type=MESH,
        ).start()

    def fault_sender(x, y):
        pltpu.make_async_remote_copy(
            src_ref=fault_out.at[x * span_y + y],
            dst_ref=fault_in.at[me],
            send_sem=block_ssem.at[0],
            recv_sem=block_rsem.at[0],
            device_id=(x, y),
            device_id_type=MESH,
        ).start()

    def await_all(buffer, sem):
        span = buffer.at[pl.ds(0, devices - 1)]
        pltpu.make_async_copy(span, span, sem).wait()

    for load in loads:
        load.wait()

    fields = jnp.concatenate(
        [
            p_ref[...],
            m_ref[...],
            trans_ref[0 : 2 * width, :],
            up_ref[0 : 2 * width, :].astype(F32),
        ],
        0,
    )
    nfield = fields.shape[0]
    spread = one_hot((iota((cells, width), 0) & (width - 1)) == iota((cells, width), 1))
    crossed = lax.dot_general(
        jnp.concatenate([spread] * 3, 1),
        jnp.concatenate(split(fields, 3), 1),
        NT,
        preferred_element_type=F32,
    )
    same = (iota((cells, nfield), 1) & (width - 1)) == (iota((cells, nfield), 0) >> shift)
    kind = iota((nfield, LANES), 0) >> shift
    lane_of = jnp.where(
        kind == 0,
        lane_p,
        jnp.where(kind <= count, (kind - 1) * count, kind - (count + 1) + lane_t),
    )
    sorter = one_hot(iota((nfield, LANES), 1) == lane_of)
    misc = jnp.dot(
        jnp.concatenate(split(jnp.where(same, crossed, 0.0), 3), 1),
        jnp.concatenate([sorter] * 3, 0),
        preferred_element_type=F32,
    )
    state_m[...] = misc
    state_l[...] = jnp.zeros_like(state_l)
    state_l[:, 0:entries] = deriv_ref[...]
    deriv = state_l[...]

    last = cells - width
    halo_out[0, 0:width] = deriv[0:width]
    halo_out[0, width : 2 * width] = misc[0:width]
    halo_out[1, 0:width] = deriv[last:]
    halo_out[1, width : 2 * width] = misc[last:]
    for side, start in ((2, 0), (3, width - 1)):
        halo_out[side, 0:width] = state_l[pl.ds(start, width, stride=width), :]
        halo_out[side, width : 2 * width] = state_m[pl.ds(start, width, stride=width), :]

    ends = (tx > 0, tx < span_x - 1, ty > 0, ty < span_y - 1)
    targets = ((tx - 1, ty), (tx + 1, ty), (tx, ty - 1), (tx, ty + 1))

    def halo_copy(side):
        return pltpu.make_async_remote_copy(
            src_ref=halo_out.at[side],
            dst_ref=halo_in.at[side ^ 1],
            send_sem=halo_ssem.at[side],
            recv_sem=halo_rsem.at[side ^ 1],
            device_id=targets[side],
            device_id_type=MESH,
        )

    caps = fsend_ref.shape[0]
    slab = fault_out.shape[1]
    lines = devices * slab
    slab_shift = slab.bit_length() - 1
    widen = one_hot((iota((lines, devices), 0) >> slab_shift) == iota((lines, devices), 1))
    picks = lax.dot_general(
        widen, fsend_ref[...].astype(F32).astype(BF16), NT, preferred_element_type=F32
    )
    part = iota((lines, 1), 0) & (slab - 1)
    index = jnp.where((part & 1) == 0, picks[:, 0:1], picks[:, 1:2])
    hit = iota((lines, cells), 1).astype(F32) == index
    take_l = one_hot(hit & (part < caps))
    take_m = one_hot(hit & (part >= caps))
    gathered = joined(
        jnp.dot(take_l, jnp.concatenate(split(deriv, 2), 1), preferred_element_type=F32), 2
    ) + joined(
        jnp.dot(take_m, jnp.concatenate(split(misc, 3), 1), preferred_element_type=F32), 3
    )
    fault_out[...] = gathered.reshape(devices, slab, LANES)
    fault_in[pl.ds(me, 1)] = fault_out[pl.ds(me, 1)]


    owner = owner_ref[...]
    named = (iota((devices, cells), 0) == owner).astype(F32)
    before = one_hot(iota((cells, cells), 0) < iota((cells, cells), 1))
    earlier = jnp.dot(named.astype(BF16), before, preferred_element_type=F32)
    rank = jnp.sum(earlier * named, 0, keepdims=True)
    slot = owner.astype(F32) * ROWS + rank
    slots = devices * ROWS
    mover = one_hot(iota((slots, cells), 0).astype(F32) == slot)

    faults = fcell_ref.shape[1]
    chosen = (iota((cells, faults), 0) == fcell_ref[...]).astype(F32)
    fslot = fslot_ref[...]
    line = lax.div(fslot, caps) * slab + lax.rem(fslot, caps)

    def of_cell(values):
        return jnp.sum(chosen * values, 1, keepdims=True)

    base = of_cell(line.astype(F32))
    fault_conduct = of_cell(ftrans_ref[...])
    fault_flag = of_cell(fup_ref[...].astype(F32))
    where = iota((cells, lines), 1).astype(F32)
    pull_l = one_hot(where == base)
    pull_m = one_hot(where == base + caps)

    row = iota((cells, 1), 0)
    at_x = row >> shift
    at_y = row & (width - 1)

    def column(array, lane):
        return array[:, lane : lane + 1]

    def terms(own_l, own_m, other_l, other_m, conduct, flag):
        lower = 1.0 - flag
        diff = column(own_m, lane_p) - column(other_m, lane_p)
        mu = (conduct * flag) * own_m + (conduct * lower) * other_m
        off = (conduct * lower * diff) * other_l - mu
        return (conduct * flag * diff) * own_l + mu, off

    for kept, field in ((near_l, deriv), (near_m, misc)):
        kept[0, width:] = field[:last]
        kept[0, 0:width] = jnp.zeros((width, LANES), F32)
        kept[1, 0:last] = field[width:]
        kept[1, last:] = jnp.zeros((width, LANES), F32)
        kept[2] = pltpu.roll(field, 1, 0)
        kept[3] = pltpu.roll(field, cells - 1, 0)
    inside = (at_x > 0, at_x < width - 1, at_y > 0, at_y < width - 1)
    for side in range(4):
        axis = side // 2
        if side % 2:
            conduct, flag = column(misc, lane_t + axis), column(misc, lane_w + axis)
        else:
            lower_m = near_m[side]
            conduct = column(lower_m, lane_t + axis)
            flag = 1.0 - column(lower_m, lane_w + axis)
        rates[side, :, 0:1] = jnp.where(inside[side], conduct, 0.0)
        rates[side, :, 1:2] = flag
    total[...] = jnp.zeros_like(total)
    total[:, 0:entries] = acc_ref[...]

    def inner(side, carry):
        rate = rates[side]
        added, off = terms(
            state_l[...],
            state_m[...],
            near_l[side],
            near_m[side],
            column(rate, 0),
            column(rate, 1),
        )
        total[...] += added
        offs[side] = off
        return carry

    pl.semaphore_wait(barrier, devices - 1)
    for side in range(4):
        pl.when(ends[side])(lambda side=side: halo_copy(side).start())
    each(fault_sender)
    lax.fori_loop(0, 4, inner, 0)

    for side in range(4):
        @pl.when(ends[side])
        def _(side=side):
            halo_copy(side ^ 1).wait_recv()

        @pl.when(jnp.logical_not(ends[side]))
        def _(side=side):
            halo_in[side] = jnp.zeros_like(halo_in[side])

    for side, rows in enumerate(
        (
            pl.ds(0, width),
            pl.ds(last, width),
            pl.ds(0, width, stride=width),
            pl.ds(width - 1, width, stride=width),
        )
    ):
        axis = side // 2
        own_l, own_m = state_l[rows, :], state_m[rows, :]
        other_l = halo_in[side, 0:width]
        other_m = halo_in[side, width : 2 * width]
        if side % 2:
            conduct = column(own_m, lane_t + axis) * jnp.where(ends[side], 1.0, 0.0)
            flag = column(own_m, lane_w + axis)
        else:
            conduct = column(other_m, lane_t + axis)
            flag = 1.0 - column(other_m, lane_w + axis)
        added, off = terms(own_l, own_m, other_l, other_m, conduct, flag)
        total[rows, :] = total[rows, :] + added
        offs[side, rows, :] = off

    def place_rows(parts, first):
        moved = jnp.dot(
            mover, jnp.concatenate(parts, 1), preferred_element_type=F32
        ).astype(BF16)
        for i in range(len(parts)):
            start = (first + i) * ROWS
            send[:, start : start + ROWS, :] = moved[:, i * LANES : (i + 1) * LANES].reshape(
                devices, ROWS, LANES
            )

    early = 4 * ROWS
    late = 2 * ROWS
    place_rows([offs[side].astype(BF16) for side in range(4)], 0)
    each_across(row_sender(0, early))

    await_all(fault_in, block_rsem.at[0])
    arrived = fault_in[...].reshape(lines, LANES)
    pieces = split(arrived, 3)
    other_l = joined(
        jnp.dot(pull_l, jnp.concatenate(pieces[:2], 1), preferred_element_type=F32), 2
    )
    other_m = joined(
        jnp.dot(pull_m, jnp.concatenate(pieces, 1), preferred_element_type=F32), 3
    )
    added, off = terms(
        state_l[...], state_m[...], other_l, other_m, fault_conduct, fault_flag
    )
    place_rows([(total[...] + added).astype(BF16), off.astype(BF16)], 4)
    each_across(row_sender(early, late))
    each_near(row_sender(0, early + late))
    own = pltpu.make_async_copy(send.at[me], land.at[me], own_sem.at[0])
    own.start()

    for side in range(4):
        pl.when(ends[side])(lambda side=side: halo_copy(side).wait_send())
    await_all(fault_out, block_ssem.at[0])
    await_all(send, block_ssem.at[1])
    own.wait()
    await_all(land, block_rsem.at[1])


def expand_kernel(capacity, count, group, land, out_ref):
    kinds = land.shape[1] // ROWS
    tall = capacity * BLOCKS
    kind = iota((tall, kinds * ROWS), 1) // ROWS
    block = jnp.where(kind < 4, kind + 1, jnp.where(kind == 4, 0, BLOCKS - 1))
    rank = iota((tall, kinds * ROWS), 1) % ROWS
    line = iota((tall, kinds * ROWS), 0)
    order = one_hot((line // BLOCKS == rank) & (line % BLOCKS == block))
    entry = iota((LANES, PAD * PAD), 0)
    target = entry // count * PAD + entry % count
    widen = one_hot((iota((LANES, PAD * PAD), 1) == target) & (entry < count * count))
    first = pl.program_id(0) * group
    ordered = []
    for i in range(0, group, 2):
        pair = jnp.concatenate([land[first + i], land[first + i + 1]], 1)
        both = jnp.dot(order, pair, preferred_element_type=F32).astype(BF16)
        ordered += [both[:, :LANES], both[:, LANES:]]
    full = jnp.dot(jnp.concatenate(ordered, 0), widen, preferred_element_type=F32)
    out_ref[...] = full.reshape(group * capacity, BLOCKS, PAD * PAD).astype(BF16)


def body(
    span_x,
    span_y,
    pressure,
    mobility,
    mob_deriv,
    accum,
    trans,
    upwind,
    fault_send,
    fault_cell,
    fault_slot,
    fault_trans,
    fault_up,
    cell_owner,
):
    width = pressure.shape[0]
    count = mobility.shape[0]
    cells = width * width
    devices = span_x * span_y
    capacity = max(2, 2 * cells // devices)
    caps = fault_send.shape[2]
    assert pressure.shape == (width, width, 1) and caps == 2
    entries = count * count
    vmem = pl.BlockSpec(memory_space=pltpu.VMEM)
    wide = pltpu.VMEM((cells, LANES), F32)
    sems = pltpu.SemaphoreType.DMA
    arrays = (
        pressure.reshape(width, width),
        mobility.reshape(count * width, width),
        jnp.transpose(mob_deriv, (1, 2, 3, 0)).reshape(cells, entries),
        jnp.transpose(accum, (1, 2, 3, 0)).reshape(cells, entries),
        trans.reshape(3 * width, width),
        upwind.reshape(3 * width, width),
        jnp.transpose(fault_send, (0, 2, 1)).reshape(caps, devices),
        fault_cell,
        fault_slot,
        fault_trans,
        fault_up,
        cell_owner.reshape(1, cells),
    )
    land = pl.pallas_call(
        functools.partial(build_kernel, span_x, span_y, width, count),
        out_shape=pltpu.VMEM((devices, 6 * ROWS, LANES), BF16),
        in_specs=[pl.BlockSpec(memory_space=pltpu.HBM)] * 12,
        out_specs=vmem,
        scratch_shapes=[pltpu.VMEM(array.shape, array.dtype) for array in arrays]
        + [wide] * 2
        + [pltpu.VMEM((4, cells, LANES), F32)] * 4
        + [wide]
        + [
            pltpu.VMEM((4, 2 * width, LANES), F32),
            pltpu.VMEM((4, 2 * width, LANES), F32),
            pltpu.VMEM((devices, 2 * caps, LANES), F32),
            pltpu.VMEM((devices, 2 * caps, LANES), F32),
            pltpu.VMEM((devices, 6 * ROWS, LANES), BF16),
            sems((len(arrays),)),
            sems((4,)),
            sems((4,)),
            sems((2,)),
            sems((2,)),
            sems((1,)),
        ],
        compiler_params=pltpu.CompilerParams(
            collective_id=0, has_side_effects=True, vmem_limit_bytes=VMEM_LIMIT
        ),
        name="build_rows",
    )(*[pltpu.with_memory_space_constraint(array, pltpu.HBM) for array in arrays])
    group = devices // 4
    full = (devices * capacity, BLOCKS, PAD * PAD)
    return pl.pallas_call(
        functools.partial(expand_kernel, capacity, count, group),
        grid=(devices // group,),
        out_shape=jax.ShapeDtypeStruct(full, BF16),
        in_specs=[vmem],
        out_specs=pl.BlockSpec((group * capacity,) + full[1:], lambda i: (i, 0, 0)),
        compiler_params=pltpu.CompilerParams(vmem_limit_bytes=EXPAND_LIMIT),
        name="expand_rows",
    )(land)


def solution(mesh):
    in_specs = (
        P("tx", "ty", None),
        P(None, "tx", "ty", None),
        P(None, "tx", "ty", None),
        P(None, "tx", "ty", None),
        P(None, "tx", "ty", None),
        P(None, "tx", "ty", None),
        P(("tx", "ty"), None, None),
        P(("tx", "ty"), None),
        P(("tx", "ty"), None),
        P(("tx", "ty"), None),
        P(("tx", "ty"), None),
        P(("tx", "ty"), None),
    )
    out_specs = P(("tx", "ty"), None, None)
    local = functools.partial(body, mesh.shape["tx"], mesh.shape["ty"])
    return jax.shard_map(local, mesh=mesh, in_specs=in_specs, out_specs=out_specs, check_vma=False)
```
